512 devices in a mesh: wide: 64 (over x_lo, z, core), narrow: 8 (over y, x_hi).
Axes of the slice: x: 4 (x_hi: 2, x_lo: 2; x = x_hi * 2 + x_lo), y: 4, z: 16, core: 2. Of those that a mesh axis runs over, the one named last changes fastest.
Arguments:
- grad_out: bfloat16 [896, 28672], P('wide', 'narrow'), may hold values from -6 to 6
- inputs: bfloat16 [896, 8192], P(None, 'wide'), may hold values from -16 to 16
- out_basis: bfloat16 [28672, 28672], P('narrow', 'wide'), may hold values from -0.03125 to 0.03125
- in_basis: bfloat16 [8192, 8192], P('wide', 'narrow'), may hold values from -0.0625 to 0.0625
- eigen_values: bfloat16 [28672, 8192], P('wide', 'narrow'), may hold values from 1e-05 to 1500
Outputs:
- scores: float32 [4, 384], replicated
The draws below stay inside these ranges and needn't reach their ends.
All inputs are finite; a program needn't handle non-finite values.
Results may differ from the reference program's by a relative error of at most 0.02.
Values may be sent and summed in bfloat16 or wider, within the bound.
No kernel may reach another device: no remote copies, remote signals or barrier semaphores. Data moves between devices by JAX's collectives and lax.ppermute only.
A program may use at most 64 MiB of HBM per device.

```python
import math
import jax
import jax.numpy as jnp
from jax import lax

D = 8192
FF = 28672
QUERIES = 4
QTOK = 128
TOKENS = 896


def draw_eigen_values(key, part):
    key = jax.random.fold_in(key, 7)
    keys = jax.random.split(key, 3)
    out_pos = jnp.arange(FF, dtype=jnp.float32) / FF
    in_pos = jnp.arange(D, dtype=jnp.float32) / D
    out_scale = jnp.power(10.0, 1.0 - 3.0 * out_pos) * jnp.exp(jax.random.uniform(keys[0], (FF,), jnp.float32, -0.7, 0.7))
    in_scale = jnp.power(10.0, 0.5 - in_pos) * jnp.exp(jax.random.uniform(keys[1], (D,), jnp.float32, -0.7, 0.7))
    correction = jnp.exp(jax.random.uniform(keys[2], (FF, D), jnp.float32, -1.0, 1.0))
    values = out_scale[:, None] * in_scale[None, :] * correction
    return values.astype(jnp.bfloat16)


def spiked(values, rng, source, target, shards_of, factor):
    def block_of(position):
        return (jnp.arange(values.shape[position]) // (values.shape[position] // shards_of)).reshape((-1,) + (1,) * (values.ndim - 1 - position))

    near = jax.random.permutation(rng, shards_of)[block_of(target)]
    other_side = (block_of(target) + shards_of // 2) % shards_of
    return jnp.where((block_of(source) == near) | (block_of(source) == other_side), factor * values, values)


def shard_levels(key, dims, cuts, least, top_value):
    loudness, own = 1.0, jax.random.fold_in(key, 6)
    for axis_at, parts in cuts:
        steps = jnp.exp(jax.random.uniform(jax.random.fold_in(own, axis_at), (parts,), jnp.float32, least / len(cuts), top_value / len(cuts)))
        loudness = loudness * jnp.repeat(steps, dims[axis_at] // parts).reshape([-1 if axis == axis_at else 1 for axis in range(len(dims))])
    return loudness


def noise(key, extent, spread, most, cuts=(), held_as=jnp.bfloat16):
    gain = shard_levels(key, extent, cuts, -0.22, 0.18) if cuts else 1.0
    result = jax.random.normal(key, extent, jnp.float32) * spread * gain
    return jnp.minimum(jnp.maximum(result, -most), most).astype(held_as)


def gaussian_with(key, shape, deviation, bound, shards, heavy, kind=jnp.bfloat16):
    values = deviation * jax.random.normal(key, shape, jnp.float32)
    if shards:
        values = values * shard_levels(key, shape, shards, -0.22, 0.18)
    return jnp.clip(spiked(values, jax.random.fold_in(key, 3), *heavy), -bound, bound).astype(kind)


def setup_inputs(seed: int = 0) -> dict:
    key_list = jax.random.split(jax.random.key(seed), 6)
    return {
        "grad_out": noise(key_list[0], (TOKENS, FF), 1.0, 6.0, ((0, 64), (1, 8))),
        "inputs": gaussian_with(key_list[1], (TOKENS, D), 1.0, 16.0, ((1, 64),), (1, 0, 64, 4.0)),
        "out_basis": noise(key_list[2], (FF, FF), FF ** -0.5, 0.03125, ((0, 8), (1, 64))),
        "in_basis": noise(key_list[3], (D, D), D ** -0.5, 0.0625, ((0, 64), (1, 8))),
        "eigen_values": draw_eigen_values(jax.random.fold_in(key_list[5], 71), 0),
    }


def reference(grad_out, inputs, out_basis, in_basis, eigen_values):
    rotated_out = jnp.dot(grad_out, out_basis, preferred_element_type=jnp.float32).astype(jnp.bfloat16)
    rotated_in = jnp.dot(inputs, in_basis, preferred_element_type=jnp.float32).astype(jnp.bfloat16)
    values = eigen_values.astype(jnp.float32)
    damping = 0.1 * jnp.sum(values) / (FF * D)
    divisor = values + damping
    query_rows = QUERIES * QTOK
    train_out = rotated_out[query_rows:].astype(jnp.float32)
    train_in = rotated_in[query_rows:]
    norm_factor = 1.0 / math.sqrt(QTOK * FF * D)

    def per_query(query):
        offset = (query * QTOK).astype(jnp.int32)
        rows_out = lax.dynamic_slice_in_dim(rotated_out, offset, QTOK, 0)
        rows_in = lax.dynamic_slice_in_dim(rotated_in, offset, QTOK, 0)
        query_grad = jnp.dot(rows_out.T, rows_in, preferred_element_type=jnp.float32)
        precond = (query_grad / divisor).astype(jnp.bfloat16)
        projected = jnp.dot(train_in, precond.T, preferred_element_type=jnp.float32)
        return lax.optimization_barrier(jnp.sum(train_out * projected, axis=1)) * norm_factor
    return lax.map(per_query, jnp.arange(QUERIES, dtype=jnp.int32))
```

```python
import math

import jax
import jax.numpy as jnp
import numpy as np
from jax import lax
from jax.experimental import pallas as pl
from jax.experimental.pallas import tpu as pltpu
from jax.sharding import Mesh, PartitionSpec as P

D = 8192
FF = 28672
QUERIES = 4
QTOK = 128
TOKENS = 896
SCORED = TOKENS - QUERIES * QTOK
X, Z, C, N = 2, 16, 2, 8
OWN = 14
ROWS = 16
RUN = Z * ROWS
HALF = X * RUN
ALL = C * HALF
PIECES = ALL // ROWS
TRAIN_Z = 2
AXES = {"x_lo": 2, "zh": 4, "zl": 4, "core": 2, "y": 4, "x_hi": 2}
ZZ = ("zh", "zl")
WIDE = ("x_lo", "zh", "zl", "core")
NARROW = ("y", "x_hi")

NEAR, MID, FAR = [0, 5, -5], [1, 6, -4, -1, 4, -6, 8], [2, 7, -3, -2, 3, -7]
OUT_HALF = [(0, z) for z in NEAR + MID] + [(1, z) for z in NEAR]
OUT_HALF += [(0, z) for z in FAR] + [(1, z) for z in MID + FAR]
SHARE = HALF // N
PER = SHARE // ROWS
OUT_ORDER = np.array([(c,) + OUT_HALF[n * PER + i] for n in range(N) for c in range(C) for i in range(PER)], np.int32)
IN_ORDER = np.array([(c, x, z) for c in range(C) for z in NEAR + MID + FAR for x in range(X)], np.int32)
OWNERS = np.array([(c, x, z) for x in range(X) for z in range(Z) for c in range(C)], np.int32)

VMEM = pl.BlockSpec(memory_space=pltpu.VMEM)
SMEM = pl.BlockSpec(memory_space=pltpu.SMEM)


def params():
    return pltpu.CompilerParams(vmem_limit_bytes=48 * 2**20)


def shift(x, axis, by):
    size = math.prod(AXES[a] for a in (axis if isinstance(axis, tuple) else (axis,)))
    return lax.ppermute(x, axis, [(i, (i + by) % size) for i in range(size)])


def from_z(x, distance):
    return shift(x, ZZ, -distance)


def cat(*parts):
    return jnp.concatenate(parts, 0)


def half(v):
    return v.astype(jnp.bfloat16)


def f32(v):
    return v.astype(jnp.float32)


def dot(a, b, over_a=1, over_b=0):
    return lax.dot_general(a, b, (((over_a,), (over_b,)), ((), ())), preferred_element_type=jnp.float32)


def rotate_in_kernel(at_ref, in_ref, basis_ref, keep_ref, send_ref, wide_s, rows_s):
    wide_s[:TOKENS, :] = f32(in_ref[...])
    wide_s[TOKENS:, :] = jnp.zeros((8, in_ref.shape[1]), jnp.float32)
    real = lax.broadcasted_iota(jnp.int32, (ROWS, 1), 0) < OWN
    for i in range(PIECES):
        block = jnp.where(real, wide_s[i * OWN:i * OWN + ROWS, :], 0.0)
        rows_s[pl.ds(pl.multiple_of(at_ref[i] * ROWS, ROWS), ROWS), :] = block
    for i in range(0, HALF, RUN):
        keep_ref[i:i + RUN, :] = dot(half(rows_s[i:i + RUN, :]), basis_ref[...])
        send_ref[i:i + RUN, :] = half(dot(half(rows_s[HALF + i:HALF + i + RUN, :]), basis_ref[...]))


def rotate_out_kernel(core_ref, *refs):
    blocks, (own_ref, other_ref, out_ref, rows_s) = refs[:6], refs[6:]
    at = 0
    for block in blocks:
        rows_s[at:at + block.shape[0], :] = block[...]
        at += block.shape[0]
    for i, basis in enumerate((own_ref, other_ref)):
        product = half(dot(rows_s[...], basis[...], 1, 1))
        out_ref[pl.ds((core_ref[0] ^ i) * HALF, HALF), :] = product


def stack_kernel(*refs):
    at = 0
    for block in refs[:-1]:
        refs[-1][at:at + block.shape[0], :] = block[...]
        at += block.shape[0]


def padding_sum(block):
    row = lax.rem(lax.broadcasted_iota(jnp.int32, block.shape, 0), ROWS)
    column = lax.broadcasted_iota(jnp.int32, block.shape, 1)
    return jnp.sum(jnp.where((row == OWN) & (column < 3), f32(block), 0.0), keepdims=True)


def with_terms(block, value):
    row = lax.broadcasted_iota(jnp.int32, block.shape, 0)
    column = lax.broadcasted_iota(jnp.int32, block.shape, 1)
    first = f32(half(value))
    second = f32(half(value - first))
    third = value - first - second
    terms = jnp.where(column == 0, first, jnp.where(column == 1, second, jnp.where(column == 2, third, 0.0)))
    return jnp.where(row == OWN, terms, block)


def share_kernel(parts_ref, ri0_ref, ri1_ref, out_ref):
    wide_sum = padding_sum(ri0_ref[:, :128]) + padding_sum(ri1_ref[:, :128])
    shares = []
    for c in range(C):
        total = f32(parts_ref[c * N])
        for n in range(1, N):
            total += f32(parts_ref[c * N + n])
        shares.append(with_terms(total, wide_sum) if c == 0 else total)
    share = half(jnp.concatenate(shares, 1))
    for n in range(N):
        out_ref[n] = share


def query_spans(q):
    spans = []
    for x in range(X):
        lo, hi = max(q * QTOK, x * 448), min((q + 1) * QTOK, (x + 1) * 448)
        if lo < hi:
            spans.append((x, (lo - x * 448) // 28, (hi - 1 - x * 448) // 28 + 1))
    return spans


def score_kernel(to_out_ref, to_in_ref, ro_ref, ri0_ref, ri1_ref, eig_ref, out_ref, ro_s, ri_s):
    def place(scratch, at_ref, i, block):
        scratch[pl.ds(pl.multiple_of(at_ref[i] * ROWS, ROWS), ROWS), :] = block

    overall = jnp.zeros((1, 1), jnp.float32)
    width = ro_ref.shape[2] // C
    for i in range(PIECES):
        n, c, at = i // (C * PER), i // PER % C, i % PER * ROWS
        place(ro_s, to_out_ref, i, ro_ref[n, at:at + ROWS, c * width:(c + 1) * width])
        source = (ri0_ref, ri1_ref)[i // (PIECES // C)]
        at = i % (PIECES // C) * ROWS
        place(ri_s, to_in_ref, i, source[at:at + ROWS, :])
    for n in range(N):
        overall += padding_sum(ro_ref[n, :ROWS, :128])

    def rows(ref, x, c, first, last):
        base = (x * C + c) * RUN
        return ref[base + first * ROWS:base + last * ROWS, :]

    def tokens(x, c, first, last, axis):
        shape = [1, 1]
        shape[axis] = (last - first) * ROWS
        at = lax.broadcasted_iota(jnp.int32, tuple(shape), axis)
        own = lax.rem(at, ROWS)
        return jnp.where(own < OWN, x * 448 + (first + at // ROWS) * 28 + c * OWN + own, -1)

    recip = 1.0 / (f32(eig_ref[...]) + overall * (0.1 / (FF * D)))
    scored = lax.broadcasted_iota(jnp.int32, (SCORED, 1), 0) + QUERIES * QTOK
    pick = jnp.concatenate([tokens(1, c, TRAIN_Z, Z, 1) for c in range(C)], 1) == scored
    pick = half(jnp.where(pick, 1.0, 0.0))
    train_out = dot(pick, cat(*[rows(ro_s, 1, c, TRAIN_Z, Z) for c in range(C)]))
    train_in = half(dot(pick, cat(*[rows(ri_s, 1, c, TRAIN_Z, Z) for c in range(C)])))
    scale = 1.0 / math.sqrt(QTOK * FF * D)
    for q in range(QUERIES):
        outs, ins = [], []
        for x, first, last in query_spans(q):
            for c in range(C):
                token = tokens(x, c, first, last, 0)
                keep = (token >= q * QTOK) & (token < (q + 1) * QTOK)
                outs.append(half(jnp.where(keep, f32(rows(ro_s, x, c, first, last)), 0.0)))
                ins.append(rows(ri_s, x, c, first, last))
        precond = half(dot(cat(*outs), cat(*ins), 0, 0) * recip)
        projected = dot(train_in, precond, 1, 1)
        score = jnp.sum(train_out * projected, axis=1) * scale
        for n in range(N):
            out_ref[n, q, :] = score


def stack(*blocks):
    rows = sum(b.shape[0] for b in blocks)
    shape = jax.ShapeDtypeStruct((rows,) + blocks[0].shape[1:], jnp.bfloat16)
    return pl.pallas_call(
        stack_kernel,
        out_shape=shape,
        in_specs=[VMEM] * len(blocks),
        out_specs=VMEM,
        compiler_params=params(),
        cost_estimate=pl.CostEstimate(flops=0, bytes_accessed=4 * shape.size, transcendentals=0),
    )(*blocks)


def gather_z(own):
    above = from_z(own, 5)
    near = stack(own, above, from_z(own, -5))
    up, down, across = from_z(near, 1), from_z(near, -1), from_z(above, 3)
    return near, (up, down, across), (from_z(up, 1), from_z(down, -1))


def on_device(grad_out, inputs, out_basis, in_basis, eigen_values):
    x_me, c_me = lax.axis_index("x_lo"), lax.axis_index("core")
    z_me = lax.axis_index(ZZ)
    n_out, n_in = out_basis.shape[1], in_basis.shape[1]

    def places(order, core, z):
        return ((x_me ^ order[:, 1]) * C + (core ^ order[:, 0])) * Z + lax.rem(z + order[:, 2] + Z, Z)

    own_basis = out_basis.T
    other_basis = shift(own_basis, "core", 1)

    near, mid, far = gather_z(lax.optimization_barrier(jnp.pad(grad_out, ((0, ROWS - OWN), (0, 0)))))
    *mid, near_x = lax.optimization_barrier((*mid, shift(near, "x_lo", 1)))
    mid, far = stack(*mid), stack(*far)
    blocks = [near, mid, near_x, far, shift(mid, "x_lo", 1), shift(far, "x_lo", 1)]

    to_rows = ((c_me ^ OWNERS[:, 0]) * X + (x_me ^ OWNERS[:, 1])) * Z + OWNERS[:, 2]
    keep, send = pl.pallas_call(
        rotate_in_kernel,
        out_shape=(jax.ShapeDtypeStruct((HALF, n_in), jnp.float32), jax.ShapeDtypeStruct((HALF, n_in), jnp.bfloat16)),
        in_specs=[SMEM, VMEM, VMEM],
        out_specs=(VMEM, VMEM),
        scratch_shapes=[
            pltpu.VMEM((TOKENS + 8, inputs.shape[1]), jnp.float32),
            pltpu.VMEM((ALL, inputs.shape[1]), jnp.float32),
        ],
        compiler_params=params(),
        cost_estimate=pl.CostEstimate(flops=3 * 10**8, bytes_accessed=3 * 10**6, transcendentals=0),
    )(to_rows, inputs, in_basis)
    part = keep + f32(shift(send, "core", 1))
    part = part[:RUN] + f32(shift(half(part[RUN:]), "x_lo", 1))
    pieces = lax.all_to_all(half(part), ZZ, 0, 0, tiled=True)
    own_in = jnp.sum(f32(pieces.reshape(Z, ROWS, n_in)), 0)
    own_in = half(with_terms(own_in, jnp.sum(eigen_values, dtype=jnp.float32)))
    near, mid, far = gather_z(cat(own_in, shift(own_in, "x_lo", 1)))
    ri0 = stack(near, *mid, *far)
    ri1 = shift(ri0, "core", 1)

    partial_out = pl.pallas_call(
        rotate_out_kernel,
        out_shape=jax.ShapeDtypeStruct((ALL, n_out), jnp.bfloat16),
        in_specs=[SMEM] + [VMEM] * 8,
        out_specs=VMEM,
        scratch_shapes=[pltpu.VMEM((HALF, grad_out.shape[1]), jnp.bfloat16)],
        compiler_params=params(),
        cost_estimate=pl.CostEstimate(flops=33 * 10**8, bytes_accessed=10**7, transcendentals=0),
    )(c_me.astype(jnp.int32).reshape(1), *blocks, own_basis, other_basis)
    parts = lax.all_to_all(partial_out, ("core",) + NARROW, 0, 0, tiled=True)
    shares = pl.pallas_call(
        share_kernel,
        out_shape=jax.ShapeDtypeStruct((N, SHARE, C * n_out), jnp.bfloat16),
        in_specs=[VMEM] * 3,
        out_specs=VMEM,
        compiler_params=params(),
        cost_estimate=pl.CostEstimate(flops=10**6, bytes_accessed=2 * 10**6, transcendentals=0),
    )(parts.reshape(C * N, SHARE, n_out), ri0, ri1)
    rotated_out = lax.all_to_all(shares, NARROW, 0, 0, tiled=True)

    scores = pl.pallas_call(
        score_kernel,
        out_shape=jax.ShapeDtypeStruct((N, QUERIES, SCORED), jnp.float32),
        in_specs=[SMEM] * 2 + [VMEM] * 4,
        out_specs=VMEM,
        scratch_shapes=[pltpu.VMEM((ALL, n_out), jnp.bfloat16), pltpu.VMEM((ALL, n_in), jnp.bfloat16)],
        compiler_params=params(),
        cost_estimate=pl.CostEstimate(flops=3 * 10**9, bytes_accessed=5 * 10**6, transcendentals=0),
    )(places(OUT_ORDER, 0, z_me), places(IN_ORDER, c_me, z_me), rotated_out, ri0, ri1, eigen_values)
    scores = jnp.sum(lax.all_to_all(scores, NARROW, 0, 0, tiled=True), 0)
    for axes in (("zl", "core"), ("x_lo", "zh")):
        scores = jnp.sum(lax.all_to_all(jnp.broadcast_to(scores, (8,) + scores.shape), axes, 0, 0, tiled=True), 0)
    return scores


def solution(mesh):
    fine = Mesh(mesh.devices.reshape(tuple(AXES.values())), tuple(AXES))
    return jax.shard_map(
        on_device,
        mesh=fine,
        in_specs=(
            P(WIDE, NARROW),
            P(None, WIDE),
            P(NARROW, WIDE),
            P(WIDE, NARROW),
            P(WIDE, NARROW),
        ),
        out_specs=P(),
        check_vma=False,
    )
```

```python
import math

import jax
import jax.numpy as jnp
import numpy as np
from jax import lax
from jax.experimental import pallas as pl
from jax.experimental.pallas import tpu as pltpu
from jax.sharding import Mesh, PartitionSpec as P

D = 8192
FF = 28672
QUERIES = 4
QTOK = 128
TOKENS = 896
SCORED = TOKENS - QUERIES * QTOK
X, Z, C, N = 2, 16, 2, 8
OWN = 14
ROWS = 16
RUN = Z * ROWS
HALF = X * RUN
ALL = C * HALF
PIECES = ALL // ROWS
TRAIN_Z = 2
AXES = {"x_lo": 2, "zh": 4, "zl": 4, "core": 2, "y": 4, "x_hi": 2}
ZZ = ("zh", "zl")
WIDE = ("x_lo", "zh", "zl", "core")
NARROW = ("y", "x_hi")

NEAR, MID, FAR = [0, 5, -5], [1, 6, -4, -1, 4, -6], [8, 2, 7, -3, -2, 3, -7]
OUT_HALF = [(0, z) for z in NEAR + MID] + [(1, z) for z in NEAR]
OUT_HALF += [(0, z) for z in FAR] + [(1, z) for z in MID + FAR]
SHARE = HALF // N
PER = SHARE // ROWS
OUT_ORDER = np.array([(c,) + OUT_HALF[n * PER + i] for n in range(N) for c in range(C) for i in range(PER)], np.int32)
IN_ORDER = np.array([(c, x, z) for c in range(C) for x in range(X) for z in range(Z)], np.int32)
OWNERS = np.array([(c, x, z) for x in range(X) for z in range(Z) for c in range(C)], np.int32)

VMEM = pl.BlockSpec(memory_space=pltpu.VMEM)
SMEM = pl.BlockSpec(memory_space=pltpu.SMEM)


def params():
    return pltpu.CompilerParams(vmem_limit_bytes=48 * 2**20)


def shift(x, axis, by):
    size = math.prod(AXES[a] for a in (axis if isinstance(axis, tuple) else (axis,)))
    return lax.ppermute(x, axis, [(i, (i + by) % size) for i in range(size)])


def from_z(x, distance):
    return shift(x, ZZ, -distance)


def cat(*parts):
    return jnp.concatenate(parts, 0)


def half(v):
    return v.astype(jnp.bfloat16)


def f32(v):
    return v.astype(jnp.float32)


def dot(a, b, over_a=1, over_b=0):
    return lax.dot_general(a, b, (((over_a,), (over_b,)), ((), ())), preferred_element_type=jnp.float32)


def rotate_in_kernel(at_ref, in_ref, basis_ref, keep_ref, send_ref, wide_s, rows_s):
    wide_s[:TOKENS, :] = f32(in_ref[...])
    wide_s[TOKENS:, :] = jnp.zeros((8, in_ref.shape[1]), jnp.float32)
    real = lax.broadcasted_iota(jnp.int32, (ROWS, 1), 0) < OWN
    for i in range(PIECES):
        block = jnp.where(real, wide_s[i * OWN:i * OWN + ROWS, :], 0.0)
        rows_s[pl.ds(pl.multiple_of(at_ref[i] * ROWS, ROWS), ROWS), :] = block
    for i in range(0, HALF, RUN):
        keep_ref[i:i + RUN, :] = dot(half(rows_s[i:i + RUN, :]), basis_ref[...])
        send_ref[i:i + RUN, :] = half(dot(half(rows_s[HALF + i:HALF + i + RUN, :]), basis_ref[...]))


def rotate_out_kernel(core_ref, *refs):
    blocks, (own_ref, other_ref, out_ref, rows_s) = refs[:6], refs[6:]
    at = 0
    for block in blocks:
        rows_s[at:at + block.shape[0], :] = block[...]
        at += block.shape[0]
    for i, basis in enumerate((own_ref, other_ref)):
        product = half(dot(rows_s[...], basis[...], 1, 1))
        out_ref[pl.ds((core_ref[0] ^ i) * HALF, HALF), :] = product


def stack_kernel(*refs):
    at = 0
    for block in refs[:-1]:
        refs[-1][at:at + block.shape[0], :] = block[...]
        at += block.shape[0]


def padding_sum(block):
    row = lax.rem(lax.broadcasted_iota(jnp.int32, block.shape, 0), ROWS)
    column = lax.broadcasted_iota(jnp.int32, block.shape, 1)
    return jnp.sum(jnp.where((row == OWN) & (column < 3), f32(block), 0.0), keepdims=True)


def with_terms(block, value):
    row = lax.broadcasted_iota(jnp.int32, block.shape, 0)
    column = lax.broadcasted_iota(jnp.int32, block.shape, 1)
    first = f32(half(value))
    second = f32(half(value - first))
    third = value - first - second
    terms = jnp.where(column == 0, first, jnp.where(column == 1, second, jnp.where(column == 2, third, 0.0)))
    return jnp.where(row == OWN, terms, block)


def share_kernel(parts_ref, out_ref):
    shares = []
    for c in range(C):
        total = f32(parts_ref[c * N])
        for n in range(1, N):
            total += f32(parts_ref[c * N + n])
        shares.append(total)
    share = half(jnp.concatenate(shares, 1))
    for n in range(N):
        out_ref[n] = share


def query_spans(q):
    spans = []
    for x in range(X):
        lo, hi = max(q * QTOK, x * 448), min((q + 1) * QTOK, (x + 1) * 448)
        if lo < hi:
            spans.append((x, (lo - x * 448) // 28, (hi - 1 - x * 448) // 28 + 1))
    return spans


def score_kernel(to_out_ref, to_in_ref, ro_ref, *refs):
    in_refs, (eig_ref, out_ref, ro_s, ri_s) = refs[:4], refs[4:]

    def place(scratch, at_ref, i, block):
        scratch[pl.ds(pl.multiple_of(at_ref[i] * ROWS, ROWS), ROWS), :] = block

    overall = sum(padding_sum(ref[:, :128]) for ref in in_refs)
    width = ro_ref.shape[2] // C
    for i in range(PIECES):
        n, c, at = i // (C * PER), i // PER % C, i % PER * ROWS
        place(ro_s, to_out_ref, i, ro_ref[n, at:at + ROWS, c * width:(c + 1) * width])
        at = i % Z * ROWS
        place(ri_s, to_in_ref, i, in_refs[i // Z][at:at + ROWS, :])

    def rows(ref, x, c, first, last):
        base = (x * C + c) * RUN
        return ref[base + first * ROWS:base + last * ROWS, :]

    def tokens(x, c, first, last, axis):
        shape = [1, 1]
        shape[axis] = (last - first) * ROWS
        at = lax.broadcasted_iota(jnp.int32, tuple(shape), axis)
        own = lax.rem(at, ROWS)
        return jnp.where(own < OWN, x * 448 + (first + at // ROWS) * 28 + c * OWN + own, -1)

    recip = 1.0 / (f32(eig_ref[...]) + overall * (0.1 / (FF * D)))
    scored = lax.broadcasted_iota(jnp.int32, (SCORED, 1), 0) + QUERIES * QTOK
    pick = jnp.concatenate([tokens(1, c, TRAIN_Z, Z, 1) for c in range(C)], 1) == scored
    pick = half(jnp.where(pick, 1.0, 0.0))
    train_out = dot(pick, cat(*[rows(ro_s, 1, c, TRAIN_Z, Z) for c in range(C)]))
    train_in = half(dot(pick, cat(*[rows(ri_s, 1, c, TRAIN_Z, Z) for c in range(C)])))
    scale = 1.0 / math.sqrt(QTOK * FF * D)
    for q in range(QUERIES):
        outs, ins = [], []
        for x, first, last in query_spans(q):
            for c in range(C):
                token = tokens(x, c, first, last, 0)
                keep = (token >= q * QTOK) & (token < (q + 1) * QTOK)
                outs.append(half(jnp.where(keep, f32(rows(ro_s, x, c, first, last)), 0.0)))
                ins.append(rows(ri_s, x, c, first, last))
        precond = half(dot(cat(*outs), cat(*ins), 0, 0) * recip)
        projected = dot(train_in, precond, 1, 1)
        score = jnp.sum(train_out * projected, axis=1) * scale
        for n in range(N):
            out_ref[n, q, :] = score


def stack(*blocks):
    rows = sum(b.shape[0] for b in blocks)
    shape = jax.ShapeDtypeStruct((rows,) + blocks[0].shape[1:], jnp.bfloat16)
    return pl.pallas_call(
        stack_kernel,
        out_shape=shape,
        in_specs=[VMEM] * len(blocks),
        out_specs=VMEM,
        compiler_params=params(),
        cost_estimate=pl.CostEstimate(flops=0, bytes_accessed=4 * shape.size, transcendentals=0),
    )(*blocks)


def on_device(grad_out, inputs, out_basis, in_basis, eigen_values):
    x_me, c_me = lax.axis_index("x_lo"), lax.axis_index("core")
    z_me = lax.axis_index(ZZ)
    n_out, n_in = out_basis.shape[1], in_basis.shape[1]

    def places(order, core, z):
        return ((x_me ^ order[:, 1]) * C + (core ^ order[:, 0])) * Z + lax.rem(z + order[:, 2] + Z, Z)

    own_basis = out_basis.T
    own, inputs = lax.optimization_barrier((jnp.pad(grad_out, ((0, ROWS - OWN), (0, 0))), inputs))
    above, below = from_z(own, 5), from_z(own, -5)
    to_rows = ((c_me ^ OWNERS[:, 0]) * X + (x_me ^ OWNERS[:, 1])) * Z + OWNERS[:, 2]
    keep, send = pl.pallas_call(
        rotate_in_kernel,
        out_shape=(jax.ShapeDtypeStruct((HALF, n_in), jnp.float32), jax.ShapeDtypeStruct((HALF, n_in), jnp.bfloat16)),
        in_specs=[SMEM, VMEM, VMEM],
        out_specs=(VMEM, VMEM),
        scratch_shapes=[
            pltpu.VMEM((TOKENS + 8, inputs.shape[1]), jnp.float32),
            pltpu.VMEM((ALL, inputs.shape[1]), jnp.float32),
        ],
        compiler_params=params(),
        cost_estimate=pl.CostEstimate(flops=3 * 10**10, bytes_accessed=3 * 10**6, transcendentals=0),
    )(to_rows, inputs, in_basis)
    part = keep + f32(shift(send, "core", 1))
    part_x = shift(half(part[RUN:]), "x_lo", 1)
    local_sum = jnp.full((N, 128), jnp.sum(eigen_values, dtype=jnp.float32))
    narrow_sum = jnp.sum(lax.all_to_all(local_sum, NARROW, 0, 0, tiled=True)[:, 0])
    above, below, part, part_x, narrow_sum = lax.optimization_barrier((above, below, part, part_x, narrow_sum))

    near = stack(own, above, below)
    up, down, near_x = from_z(near, 1), from_z(near, -1), shift(near, "x_lo", 1)
    across = from_z(above, 3)
    other_basis = shift(own_basis, "core", 1)
    part = half(part[:RUN] + f32(part_x))
    up, down, near_x, part = lax.optimization_barrier((up, down, near_x, part))
    pieces = lax.all_to_all(part, ZZ, 0, 0, tiled=True)
    mid = stack(up, down)
    *far, mid_x = lax.optimization_barrier((from_z(up, 1), from_z(down, -1), shift(mid, "x_lo", 1)))
    far = stack(across, *far)
    far_x = shift(far, "x_lo", 1)
    blocks = [near, mid, near_x, far, mid_x, far_x]

    own_in = jnp.sum(f32(pieces.reshape(Z, ROWS, n_in)), 0)
    own_in = half(with_terms(own_in, narrow_sum))
    column = lax.all_to_all(jnp.broadcast_to(own_in, (Z,) + own_in.shape), ZZ, 0, 0, tiled=True)

    partial_out = pl.pallas_call(
        rotate_out_kernel,
        out_shape=jax.ShapeDtypeStruct((ALL, n_out), jnp.bfloat16),
        in_specs=[SMEM] + [VMEM] * 8,
        out_specs=VMEM,
        scratch_shapes=[pltpu.VMEM((HALF, grad_out.shape[1]), jnp.bfloat16)],
        compiler_params=params(),
        cost_estimate=pl.CostEstimate(flops=33 * 10**8, bytes_accessed=10**7, transcendentals=0),
    )(c_me.astype(jnp.int32).reshape(1), *blocks, own_basis, other_basis)
    column, partial_out = lax.optimization_barrier((column.reshape(RUN, n_in), partial_out))
    column_x = shift(column, "x_lo", 1)
    rotated_in = [column, column_x, shift(column, "core", 1), shift(column_x, "core", 1)]

    parts = lax.all_to_all(partial_out, ("core",) + NARROW, 0, 0, tiled=True)
    shares = pl.pallas_call(
        share_kernel,
        out_shape=jax.ShapeDtypeStruct((N, SHARE, C * n_out), jnp.bfloat16),
        in_specs=[VMEM],
        out_specs=VMEM,
        compiler_params=params(),
        cost_estimate=pl.CostEstimate(flops=10**6, bytes_accessed=2 * 10**6, transcendentals=0),
    )(parts.reshape(C * N, SHARE, n_out))
    rotated_out = lax.all_to_all(shares, NARROW, 0, 0, tiled=True)

    scores = pl.pallas_call(
        score_kernel,
        out_shape=jax.ShapeDtypeStruct((N, QUERIES, SCORED), jnp.float32),
        in_specs=[SMEM] * 2 + [VMEM] * 6,
        out_specs=VMEM,
        scratch_shapes=[pltpu.VMEM((ALL, n_out), jnp.bfloat16), pltpu.VMEM((ALL, n_in), jnp.bfloat16)],
        compiler_params=params(),
        cost_estimate=pl.CostEstimate(flops=3 * 10**9, bytes_accessed=5 * 10**6, transcendentals=0),
    )(places(OUT_ORDER, 0, z_me), places(IN_ORDER, c_me, 0), rotated_out, *rotated_in, eigen_values)
    scores = jnp.sum(lax.all_to_all(scores, NARROW, 0, 0, tiled=True), 0)
    for axes in (("zl", "core"), ("x_lo", "zh")):
        scores = jnp.sum(lax.all_to_all(jnp.broadcast_to(scores, (8,) + scores.shape), axes, 0, 0, tiled=True), 0)
    return scores


def solution(mesh):
    fine = Mesh(mesh.devices.reshape(tuple(AXES.values())), tuple(AXES))
    return jax.shard_map(
        on_device,
        mesh=fine,
        in_specs=(
            P(WIDE, NARROW),
            P(None, WIDE),
            P(NARROW, WIDE),
            P(WIDE, NARROW),
            P(WIDE, NARROW),
        ),
        out_specs=P(),
        check_vma=False,
    )
```

```python
import math

import jax
import jax.numpy as jnp
import numpy as np
from jax import lax
from jax.experimental import pallas as pl
from jax.experimental.pallas import tpu as pltpu
from jax.sharding import Mesh, PartitionSpec as P

D = 8192
FF = 28672
QUERIES = 4
QTOK = 128
TOKENS = 896
SCORED = TOKENS - QUERIES * QTOK
X, Z, C, N = 2, 16, 2, 8
OWN = 14
ROWS = 16
RUN = Z * ROWS
HALF = X * RUN
ALL = C * HALF
PIECES = ALL // ROWS
TRAIN_Z = 2
AXES = {"x_lo": 2, "zh": 4, "zl": 4, "core": 2, "y": 4, "x_hi": 2}
ZZ = ("zh", "zl")
WIDE = ("x_lo", "zh", "zl", "core")
NARROW = ("y", "x_hi")

NEAR, MID, FAR = [0, 5, -5], [1, 6, -4, -1, 4, -6], [8, 2, 7, -3, -2, 3, -7]
OUT_HALF = [(0, z) for z in NEAR + MID] + [(1, z) for z in NEAR]
OUT_HALF += [(0, z) for z in FAR] + [(1, z) for z in MID + FAR]
SHARE = HALF // N
PER = SHARE // ROWS
OUT_ORDER = np.array([(c,) + OUT_HALF[n * PER + i] for n in range(N) for c in range(C) for i in range(PER)], np.int32)
IN_ORDER = np.array([(c, x, z) for c in range(C) for x in range(X) for z in range(Z)], np.int32)
OWNERS = np.array([(c, x, z) for x in range(X) for z in range(Z) for c in range(C)], np.int32)

VMEM = pl.BlockSpec(memory_space=pltpu.VMEM)
SMEM = pl.BlockSpec(memory_space=pltpu.SMEM)


def params():
    return pltpu.CompilerParams(vmem_limit_bytes=48 * 2**20)


def shift(x, axis, by):
    size = math.prod(AXES[a] for a in (axis if isinstance(axis, tuple) else (axis,)))
    return lax.ppermute(x, axis, [(i, (i + by) % size) for i in range(size)])


def from_z(x, distance):
    return shift(x, ZZ, -distance)


def cat(*parts):
    return jnp.concatenate(parts, 0)


def half(v):
    return v.astype(jnp.bfloat16)


def f32(v):
    return v.astype(jnp.float32)


def dot(a, b, over_a=1, over_b=0):
    return lax.dot_general(a, b, (((over_a,), (over_b,)), ((), ())), preferred_element_type=jnp.float32)


def rotate_in_kernel(at_ref, in_ref, basis_ref, keep_ref, send_ref, wide_s, rows_s):
    wide_s[:TOKENS, :] = f32(in_ref[...])
    wide_s[TOKENS:, :] = jnp.zeros((8, in_ref.shape[1]), jnp.float32)
    real = lax.broadcasted_iota(jnp.int32, (ROWS, 1), 0) < OWN
    for i in range(PIECES):
        block = jnp.where(real, wide_s[i * OWN:i * OWN + ROWS, :], 0.0)
        rows_s[pl.ds(pl.multiple_of(at_ref[i] * ROWS, ROWS), ROWS), :] = block
    for i in range(0, HALF, RUN):
        keep_ref[i:i + RUN, :] = dot(half(rows_s[i:i + RUN, :]), basis_ref[...])
        send_ref[i:i + RUN, :] = half(dot(half(rows_s[HALF + i:HALF + i + RUN, :]), basis_ref[...]))


def rotate_out_kernel(core_ref, *refs):
    blocks, (own_ref, other_ref, out_ref, rows_s) = refs[:6], refs[6:]
    at = 0
    for block in blocks:
        rows_s[at:at + block.shape[0], :] = block[...]
        at += block.shape[0]
    for i, basis in enumerate((own_ref, other_ref)):
        product = half(dot(rows_s[...], basis[...], 1, 1))
        out_ref[pl.ds((core_ref[0] ^ i) * HALF, HALF), :] = product


def stack_kernel(*refs):
    at = 0
    for block in refs[:-1]:
        refs[-1][at:at + block.shape[0], :] = block[...]
        at += block.shape[0]


def padding_sum(block):
    row = lax.rem(lax.broadcasted_iota(jnp.int32, block.shape, 0), ROWS)
    column = lax.broadcasted_iota(jnp.int32, block.shape, 1)
    return jnp.sum(jnp.where((row == OWN) & (column < 3), f32(block), 0.0), keepdims=True)


def with_terms(block, value):
    row = lax.broadcasted_iota(jnp.int32, block.shape, 0)
    column = lax.broadcasted_iota(jnp.int32, block.shape, 1)
    first = f32(half(value))
    second = f32(half(value - first))
    third = value - first - second
    terms = jnp.where(column == 0, first, jnp.where(column == 1, second, jnp.where(column == 2, third, 0.0)))
    return jnp.where(row == OWN, terms, block)


def share_kernel(parts_ref, out_ref):
    shares = []
    for c in range(C):
        total = f32(parts_ref[c * N])
        for n in range(1, N):
            total += f32(parts_ref[c * N + n])
        shares.append(total)
    share = half(jnp.concatenate(shares, 1))
    for n in range(N):
        out_ref[n] = share


def query_spans(q):
    spans = []
    for x in range(X):
        lo, hi = max(q * QTOK, x * 448), min((q + 1) * QTOK, (x + 1) * 448)
        if lo < hi:
            spans.append((x, (lo - x * 448) // 28, (hi - 1 - x * 448) // 28 + 1))
    return spans


def score_kernel(to_out_ref, to_in_ref, ro_ref, *refs):
    in_refs, (eig_ref, out_ref, ro_s, ri_s) = refs[:4], refs[4:]

    def place(scratch, at_ref, i, block):
        scratch[pl.ds(pl.multiple_of(at_ref[i] * ROWS, ROWS), ROWS), :] = block

    overall = sum(padding_sum(ref[:, :128]) for ref in in_refs)
    width = ro_ref.shape[2] // C
    for i in range(PIECES):
        n, c, at = i // (C * PER), i // PER % C, i % PER * ROWS
        place(ro_s, to_out_ref, i, ro_ref[n, at:at + ROWS, c * width:(c + 1) * width])
        at = i % Z * ROWS
        place(ri_s, to_in_ref, i, in_refs[i // Z][at:at + ROWS, :])

    def rows(ref, x, c, first, last):
        base = (x * C + c) * RUN
        return ref[base + first * ROWS:base + last * ROWS, :]

    def tokens(x, c, first, last, axis):
        shape = [1, 1]
        shape[axis] = (last - first) * ROWS
        at = lax.broadcasted_iota(jnp.int32, tuple(shape), axis)
        own = lax.rem(at, ROWS)
        return jnp.where(own < OWN, x * 448 + (first + at // ROWS) * 28 + c * OWN + own, -1)

    recip = 1.0 / (f32(eig_ref[...]) + overall * (0.1 / (FF * D)))
    scored = lax.broadcasted_iota(jnp.int32, (SCORED, 1), 0) + QUERIES * QTOK
    pick = jnp.concatenate([tokens(1, c, TRAIN_Z, Z, 1) for c in range(C)], 1) == scored
    pick = half(jnp.where(pick, 1.0, 0.0))
    train_out = dot(pick, cat(*[rows(ro_s, 1, c, TRAIN_Z, Z) for c in range(C)]))
    train_in = half(dot(pick, cat(*[rows(ri_s, 1, c, TRAIN_Z, Z) for c in range(C)])))
    scale = 1.0 / math.sqrt(QTOK * FF * D)
    for q in range(QUERIES):
        outs, ins = [], []
        for x, first, last in query_spans(q):
            for c in range(C):
                token = tokens(x, c, first, last, 0)
                keep = (token >= q * QTOK) & (token < (q + 1) * QTOK)
                outs.append(half(jnp.where(keep, f32(rows(ro_s, x, c, first, last)), 0.0)))
                ins.append(rows(ri_s, x, c, first, last))
        precond = half(dot(cat(*outs), cat(*ins), 0, 0) * recip)
        projected = dot(train_in, precond, 1, 1)
        score = jnp.sum(train_out * projected, axis=1) * scale
        for n in range(N):
            out_ref[n, q, :] = score


def stack(*blocks):
    rows = sum(b.shape[0] for b in blocks)
    shape = jax.ShapeDtypeStruct((rows,) + blocks[0].shape[1:], jnp.bfloat16)
    return pl.pallas_call(
        stack_kernel,
        out_shape=shape,
        in_specs=[VMEM] * len(blocks),
        out_specs=VMEM,
        compiler_params=params(),
        cost_estimate=pl.CostEstimate(flops=0, bytes_accessed=4 * shape.size, transcendentals=0),
    )(*blocks)


def on_device(grad_out, inputs, out_basis, in_basis, eigen_values):
    x_me, c_me = lax.axis_index("x_lo"), lax.axis_index("core")
    z_me = lax.axis_index(ZZ)
    n_out, n_in = out_basis.shape[1], in_basis.shape[1]

    def places(order, core, z):
        return ((x_me ^ order[:, 1]) * C + (core ^ order[:, 0])) * Z + lax.rem(z + order[:, 2] + Z, Z)

    own_basis = out_basis.T
    own = lax.optimization_barrier(jnp.pad(grad_out, ((0, ROWS - OWN), (0, 0))))
    above, below = from_z(own, 5), from_z(own, -5)
    above, below, inputs, eigen_values = lax.optimization_barrier((above, below, inputs, eigen_values))
    to_rows = ((c_me ^ OWNERS[:, 0]) * X + (x_me ^ OWNERS[:, 1])) * Z + OWNERS[:, 2]
    keep, send = pl.pallas_call(
        rotate_in_kernel,
        out_shape=(jax.ShapeDtypeStruct((HALF, n_in), jnp.float32), jax.ShapeDtypeStruct((HALF, n_in), jnp.bfloat16)),
        in_specs=[SMEM, VMEM, VMEM],
        out_specs=(VMEM, VMEM),
        scratch_shapes=[
            pltpu.VMEM((TOKENS + 8, inputs.shape[1]), jnp.float32),
            pltpu.VMEM((ALL, inputs.shape[1]), jnp.float32),
        ],
        compiler_params=params(),
        cost_estimate=pl.CostEstimate(flops=3 * 10**8, bytes_accessed=3 * 10**6, transcendentals=0),
    )(to_rows, inputs, in_basis)
    part = keep + f32(shift(send, "core", 1))
    local_sum = jnp.full((N, 128), jnp.sum(eigen_values, dtype=jnp.float32))
    narrow_sum = jnp.sum(lax.all_to_all(local_sum, NARROW, 0, 0, tiled=True)[:, 0])

    near = stack(own, above, below)
    up, down, near_x = from_z(near, 1), from_z(near, -1), shift(near, "x_lo", 1)
    across = from_z(above, 3)
    other_basis = shift(own_basis, "core", 1)
    part = half(part[:RUN] + f32(shift(half(part[RUN:]), "x_lo", 1)))
    up, down, near_x, across, narrow_sum = lax.optimization_barrier((up, down, near_x, across, narrow_sum))
    mid = stack(up, down)
    *far, mid_x, part = lax.optimization_barrier((from_z(up, 1), from_z(down, -1), shift(mid, "x_lo", 1), part))
    far, part = lax.optimization_barrier((stack(across, *far), part))
    far_x = shift(far, "x_lo", 1)
    blocks = [near, mid, near_x, far, mid_x, far_x]

    pieces = lax.all_to_all(part, ZZ, 0, 0, tiled=True)
    partial_out = pl.pallas_call(
        rotate_out_kernel,
        out_shape=jax.ShapeDtypeStruct((ALL, n_out), jnp.bfloat16),
        in_specs=[SMEM] + [VMEM] * 8,
        out_specs=VMEM,
        scratch_shapes=[pltpu.VMEM((HALF, grad_out.shape[1]), jnp.bfloat16)],
        compiler_params=params(),
        cost_estimate=pl.CostEstimate(flops=33 * 10**8, bytes_accessed=10**7, transcendentals=0),
    )(c_me.astype(jnp.int32).reshape(1), *blocks, own_basis, other_basis)
    pieces, partial_out = lax.optimization_barrier((pieces, partial_out))
    own_in = jnp.sum(f32(pieces.reshape(Z, ROWS, n_in)), 0)
    own_in = half(with_terms(own_in, narrow_sum))
    column = lax.all_to_all(jnp.broadcast_to(own_in, (Z,) + own_in.shape), ZZ, 0, 0, tiled=True).reshape(RUN, n_in)
    column_x = shift(column, "x_lo", 1)
    rotated_in = [column, column_x, shift(column, "core", 1), shift(column_x, "core", 1)]

    parts = lax.all_to_all(partial_out, ("core",) + NARROW, 0, 0, tiled=True)
    shares = pl.pallas_call(
        share_kernel,
        out_shape=jax.ShapeDtypeStruct((N, SHARE, C * n_out), jnp.bfloat16),
        in_specs=[VMEM],
        out_specs=VMEM,
        compiler_params=params(),
        cost_estimate=pl.CostEstimate(flops=10**6, bytes_accessed=2 * 10**6, transcendentals=0),
    )(parts.reshape(C * N, SHARE, n_out))
    rotated_out = lax.all_to_all(shares, NARROW, 0, 0, tiled=True)

    scores = pl.pallas_call(
        score_kernel,
        out_shape=jax.ShapeDtypeStruct((N, QUERIES, SCORED), jnp.float32),
        in_specs=[SMEM] * 2 + [VMEM] * 6,
        out_specs=VMEM,
        scratch_shapes=[pltpu.VMEM((ALL, n_out), jnp.bfloat16), pltpu.VMEM((ALL, n_in), jnp.bfloat16)],
        compiler_params=params(),
        cost_estimate=pl.CostEstimate(flops=3 * 10**9, bytes_accessed=5 * 10**6, transcendentals=0),
    )(places(OUT_ORDER, 0, z_me), places(IN_ORDER, c_me, 0), rotated_out, *rotated_in, eigen_values)
    scores = jnp.sum(lax.all_to_all(scores, NARROW, 0, 0, tiled=True), 0)
    for axes in (("zl", "core"), ("x_lo", "zh")):
        scores = jnp.sum(lax.all_to_all(jnp.broadcast_to(scores, (8,) + scores.shape), axes, 0, 0, tiled=True), 0)
    return scores


def solution(mesh):
    fine = Mesh(mesh.devices.reshape(tuple(AXES.values())), tuple(AXES))
    return jax.shard_map(
        on_device,
        mesh=fine,
        in_specs=(
            P(WIDE, NARROW),
            P(None, WIDE),
            P(NARROW, WIDE),
            P(WIDE, NARROW),
            P(WIDE, NARROW),
        ),
        out_specs=P(),
        check_vma=False,
    )
```

```python
import math

import jax
import jax.numpy as jnp
import numpy as np
from jax import lax
from jax.experimental import pallas as pl
from jax.experimental.pallas import tpu as pltpu
from jax.sharding import Mesh, PartitionSpec as P

D = 8192
FF = 28672
QUERIES = 4
QTOK = 128
TOKENS = 896
SCORED = TOKENS - QUERIES * QTOK
X, Z, C, N = 2, 16, 2, 8
OWN = 14
ROWS = 16
RUN = Z * ROWS
HALF = X * RUN
ALL = C * HALF
PIECES = ALL // ROWS
TRAIN_Z = 2
AXES = {"x_lo": 2, "zh": 4, "zl": 4, "core": 2, "y": 4, "x_hi": 2}
ZZ = ("zh", "zl")
WIDE = ("x_lo", "zh", "zl", "core")
NARROW = ("y", "x_hi")

NEAR, MID, FAR = [0, 5, -5], [1, 6, -4, -1, 4, -6], [8, 2, 7, -3, -2, 3, -7]
OUT_HALF = [(0, z) for z in NEAR + MID] + [(1, z) for z in NEAR]
OUT_HALF += [(0, z) for z in FAR] + [(1, z) for z in MID + FAR]
SHARE = HALF // N
PER = SHARE // ROWS
OUT_ORDER = np.array([(c,) + OUT_HALF[n * PER + i] for n in range(N) for c in range(C) for i in range(PER)], np.int32)
IN_ORDER = np.array([(c, x, z) for c in range(C) for x in range(X) for z in range(Z)], np.int32)
OWNERS = np.array([(c, x, z) for x in range(X) for z in range(Z) for c in range(C)], np.int32)

VMEM = pl.BlockSpec(memory_space=pltpu.VMEM)
SMEM = pl.BlockSpec(memory_space=pltpu.SMEM)


def params():
    return pltpu.CompilerParams(vmem_limit_bytes=48 * 2**20)


def shift(x, axis, by):
    size = math.prod(AXES[a] for a in (axis if isinstance(axis, tuple) else (axis,)))
    return lax.ppermute(x, axis, [(i, (i + by) % size) for i in range(size)])


def from_z(x, distance):
    return shift(x, ZZ, -distance)


def cat(*parts):
    return jnp.concatenate(parts, 0)


def half(v):
    return v.astype(jnp.bfloat16)


def f32(v):
    return v.astype(jnp.float32)


def dot(a, b, over_a=1, over_b=0):
    return lax.dot_general(a, b, (((over_a,), (over_b,)), ((), ())), preferred_element_type=jnp.float32)


def rotate_in_kernel(at_ref, in_ref, basis_ref, keep_ref, send_ref, wide_s, rows_s):
    wide_s[:TOKENS, :] = f32(in_ref[...])
    wide_s[TOKENS:, :] = jnp.zeros((8, in_ref.shape[1]), jnp.float32)
    real = lax.broadcasted_iota(jnp.int32, (ROWS, 1), 0) < OWN
    for i in range(PIECES):
        block = jnp.where(real, wide_s[i * OWN:i * OWN + ROWS, :], 0.0)
        rows_s[pl.ds(pl.multiple_of(at_ref[i] * ROWS, ROWS), ROWS), :] = block
    for i in range(0, HALF, RUN):
        keep_ref[i:i + RUN, :] = dot(half(rows_s[i:i + RUN, :]), basis_ref[...])
        send_ref[i:i + RUN, :] = half(dot(half(rows_s[HALF + i:HALF + i + RUN, :]), basis_ref[...]))


def rotate_out_kernel(core_ref, *refs):
    blocks, (own_ref, other_ref, out_ref, rows_s) = refs[:6], refs[6:]
    at = 0
    for block in blocks:
        rows_s[at:at + block.shape[0], :] = block[...]
        at += block.shape[0]
    for i, basis in enumerate((own_ref, other_ref)):
        product = half(dot(rows_s[...], basis[...], 1, 1))
        out_ref[pl.ds((core_ref[0] ^ i) * HALF, HALF), :] = product


def stack_kernel(*refs):
    at = 0
    for block in refs[:-1]:
        refs[-1][at:at + block.shape[0], :] = block[...]
        at += block.shape[0]


def padding_sum(block):
    row = lax.rem(lax.broadcasted_iota(jnp.int32, block.shape, 0), ROWS)
    column = lax.broadcasted_iota(jnp.int32, block.shape, 1)
    return jnp.sum(jnp.where((row == OWN) & (column < 3), f32(block), 0.0), keepdims=True)


def with_terms(block, value):
    row = lax.broadcasted_iota(jnp.int32, block.shape, 0)
    column = lax.broadcasted_iota(jnp.int32, block.shape, 1)
    first = f32(half(value))
    second = f32(half(value - first))
    third = value - first - second
    terms = jnp.where(column == 0, first, jnp.where(column == 1, second, jnp.where(column == 2, third, 0.0)))
    return jnp.where(row == OWN, terms, block)


def share_kernel(parts_ref, out_ref):
    shares = []
    for c in range(C):
        total = f32(parts_ref[c * N])
        for n in range(1, N):
            total += f32(parts_ref[c * N + n])
        shares.append(total)
    share = half(jnp.concatenate(shares, 1))
    for n in range(N):
        out_ref[n] = share


def query_spans(q):
    spans = []
    for x in range(X):
        lo, hi = max(q * QTOK, x * 448), min((q + 1) * QTOK, (x + 1) * 448)
        if lo < hi:
            spans.append((x, (lo - x * 448) // 28, (hi - 1 - x * 448) // 28 + 1))
    return spans


def score_kernel(to_out_ref, to_in_ref, ro_ref, *refs):
    in_refs, (eig_ref, out_ref, ro_s, ri_s) = refs[:4], refs[4:]

    def place(scratch, at_ref, i, block):
        scratch[pl.ds(pl.multiple_of(at_ref[i] * ROWS, ROWS), ROWS), :] = block

    overall = sum(padding_sum(ref[:, :128]) for ref in in_refs)
    width = ro_ref.shape[2] // C
    for i in range(PIECES):
        n, c, at = i // (C * PER), i // PER % C, i % PER * ROWS
        place(ro_s, to_out_ref, i, ro_ref[n, at:at + ROWS, c * width:(c + 1) * width])
        at = i % Z * ROWS
        place(ri_s, to_in_ref, i, in_refs[i // Z][at:at + ROWS, :])

    def rows(ref, x, c, first, last):
        base = (x * C + c) * RUN
        return ref[base + first * ROWS:base + last * ROWS, :]

    def tokens(x, c, first, last, axis):
        shape = [1, 1]
        shape[axis] = (last - first) * ROWS
        at = lax.broadcasted_iota(jnp.int32, tuple(shape), axis)
        own = lax.rem(at, ROWS)
        return jnp.where(own < OWN, x * 448 + (first + at // ROWS) * 28 + c * OWN + own, -1)

    recip = 1.0 / (f32(eig_ref[...]) + overall * (0.1 / (FF * D)))
    scored = lax.broadcasted_iota(jnp.int32, (SCORED, 1), 0) + QUERIES * QTOK
    pick = jnp.concatenate([tokens(1, c, TRAIN_Z, Z, 1) for c in range(C)], 1) == scored
    pick = half(jnp.where(pick, 1.0, 0.0))
    train_out = dot(pick, cat(*[rows(ro_s, 1, c, TRAIN_Z, Z) for c in range(C)]))
    train_in = half(dot(pick, cat(*[rows(ri_s, 1, c, TRAIN_Z, Z) for c in range(C)])))
    scale = 1.0 / math.sqrt(QTOK * FF * D)
    for q in range(QUERIES):
        outs, ins = [], []
        for x, first, last in query_spans(q):
            for c in range(C):
                token = tokens(x, c, first, last, 0)
                keep = (token >= q * QTOK) & (token < (q + 1) * QTOK)
                outs.append(half(jnp.where(keep, f32(rows(ro_s, x, c, first, last)), 0.0)))
                ins.append(rows(ri_s, x, c, first, last))
        precond = half(dot(cat(*outs), cat(*ins), 0, 0) * recip)
        projected = dot(train_in, precond, 1, 1)
        score = jnp.sum(train_out * projected, axis=1) * scale
        for n in range(N):
            out_ref[n, q, :] = score


def stack(*blocks):
    rows = sum(b.shape[0] for b in blocks)
    shape = jax.ShapeDtypeStruct((rows,) + blocks[0].shape[1:], jnp.bfloat16)
    return pl.pallas_call(
        stack_kernel,
        out_shape=shape,
        in_specs=[VMEM] * len(blocks),
        out_specs=VMEM,
        compiler_params=params(),
        cost_estimate=pl.CostEstimate(flops=0, bytes_accessed=4 * shape.size, transcendentals=0),
    )(*blocks)


def on_device(grad_out, inputs, out_basis, in_basis, eigen_values):
    x_me, c_me = lax.axis_index("x_lo"), lax.axis_index("core")
    z_me = lax.axis_index(ZZ)
    n_out, n_in = out_basis.shape[1], in_basis.shape[1]

    def places(order, core, z):
        return ((x_me ^ order[:, 1]) * C + (core ^ order[:, 0])) * Z + lax.rem(z + order[:, 2] + Z, Z)

    own_basis = out_basis.T
    own = lax.optimization_barrier(jnp.pad(grad_out, ((0, ROWS - OWN), (0, 0))))
    above, below = from_z(own, 5), from_z(own, -5)
    to_rows = ((c_me ^ OWNERS[:, 0]) * X + (x_me ^ OWNERS[:, 1])) * Z + OWNERS[:, 2]
    keep, send = pl.pallas_call(
        rotate_in_kernel,
        out_shape=(jax.ShapeDtypeStruct((HALF, n_in), jnp.float32), jax.ShapeDtypeStruct((HALF, n_in), jnp.bfloat16)),
        in_specs=[SMEM, VMEM, VMEM],
        out_specs=(VMEM, VMEM),
        scratch_shapes=[
            pltpu.VMEM((TOKENS + 8, inputs.shape[1]), jnp.float32),
            pltpu.VMEM((ALL, inputs.shape[1]), jnp.float32),
        ],
        compiler_params=params(),
        cost_estimate=pl.CostEstimate(flops=3 * 10**8, bytes_accessed=3 * 10**6, transcendentals=0),
    )(to_rows, inputs, in_basis)
    above, below, sent, eigen_values = lax.optimization_barrier((above, below, shift(send, "core", 1), eigen_values))
    part = keep + f32(sent)
    local_sum = jnp.full((N, 128), jnp.sum(eigen_values, dtype=jnp.float32))
    narrow_sum = jnp.sum(lax.all_to_all(local_sum, NARROW, 0, 0, tiled=True)[:, 0])

    near = stack(own, above, below)
    up, down, near_x = from_z(near, 1), from_z(near, -1), shift(near, "x_lo", 1)
    across = from_z(above, 3)
    other_basis = shift(own_basis, "core", 1)
    part = half(part[:RUN] + f32(shift(half(part[RUN:]), "x_lo", 1)))
    up, down, near_x = lax.optimization_barrier((up, down, near_x))
    part, _ = lax.optimization_barrier((part, up))
    mid = stack(up, down)
    *far, mid_x, narrow_sum = lax.optimization_barrier((from_z(up, 1), from_z(down, -1), shift(mid, "x_lo", 1), narrow_sum))
    far = stack(across, *far)
    far_x = shift(far, "x_lo", 1)
    blocks = [near, mid, near_x, far, mid_x, far_x]

    pieces, far = lax.optimization_barrier((lax.all_to_all(part, ZZ, 0, 0, tiled=True), far))
    blocks[3] = far
    own_in = jnp.sum(f32(pieces.reshape(Z, ROWS, n_in)), 0)
    own_in = half(with_terms(own_in, narrow_sum))
    column = lax.all_gather(own_in, ZZ, axis=0, tiled=True)
    partial_out = pl.pallas_call(
        rotate_out_kernel,
        out_shape=jax.ShapeDtypeStruct((ALL, n_out), jnp.bfloat16),
        in_specs=[SMEM] + [VMEM] * 8,
        out_specs=VMEM,
        scratch_shapes=[pltpu.VMEM((HALF, grad_out.shape[1]), jnp.bfloat16)],
        compiler_params=params(),
        cost_estimate=pl.CostEstimate(flops=33 * 10**8, bytes_accessed=10**7, transcendentals=0),
    )(c_me.astype(jnp.int32).reshape(1), *blocks, own_basis, other_basis)
    partial_out, column = lax.optimization_barrier((partial_out, column))
    parts = lax.all_to_all(partial_out, ("core",) + NARROW, 0, 0, tiled=True)
    shares = pl.pallas_call(
        share_kernel,
        out_shape=jax.ShapeDtypeStruct((N, SHARE, C * n_out), jnp.bfloat16),
        in_specs=[VMEM],
        out_specs=VMEM,
        compiler_params=params(),
        cost_estimate=pl.CostEstimate(flops=10**6, bytes_accessed=2 * 10**6, transcendentals=0),
    )(parts.reshape(C * N, SHARE, n_out))
    column_x = shift(column, "x_lo", 1)
    rotated_in = [column, column_x, shift(column, "core", 1), shift(column_x, "core", 1)]
    rotated_out = lax.all_to_all(shares, NARROW, 0, 0, tiled=True)

    scores = pl.pallas_call(
        score_kernel,
        out_shape=jax.ShapeDtypeStruct((N, QUERIES, SCORED), jnp.float32),
        in_specs=[SMEM] * 2 + [VMEM] * 6,
        out_specs=VMEM,
        scratch_shapes=[pltpu.VMEM((ALL, n_out), jnp.bfloat16), pltpu.VMEM((ALL, n_in), jnp.bfloat16)],
        compiler_params=params(),
        cost_estimate=pl.CostEstimate(flops=3 * 10**9, bytes_accessed=5 * 10**6, transcendentals=0),
    )(places(OUT_ORDER, 0, z_me), places(IN_ORDER, c_me, 0), rotated_out, *rotated_in, eigen_values)
    scores = jnp.sum(lax.all_to_all(scores, NARROW, 0, 0, tiled=True), 0)
    for axes in (("zl", "core"), ("x_lo", "zh")):
        scores = jnp.sum(lax.all_to_all(jnp.broadcast_to(scores, (8,) + scores.shape), axes, 0, 0, tiled=True), 0)
    return scores


def solution(mesh):
    fine = Mesh(mesh.devices.reshape(tuple(AXES.values())), tuple(AXES))
    return jax.shard_map(
        on_device,
        mesh=fine,
        in_specs=(
            P(WIDE, NARROW),
            P(None, WIDE),
            P(NARROW, WIDE),
            P(WIDE, NARROW),
            P(WIDE, NARROW),
        ),
        out_specs=P(),
        check_vma=False,
    )
```

```python
import math

import jax
import jax.numpy as jnp
import numpy as np
from jax import lax
from jax.experimental import pallas as pl
from jax.experimental.pallas import tpu as pltpu
from jax.sharding import Mesh, PartitionSpec as P

D = 8192
FF = 28672
QUERIES = 4
QTOK = 128
TOKENS = 896
SCORED = TOKENS - QUERIES * QTOK
X, Z, C, N = 2, 16, 2, 8
OWN = 14
ROWS = 16
RUN = Z * ROWS
HALF = X * RUN
ALL = C * HALF
PIECES = ALL // ROWS
TRAIN_Z = 2
AXES = {"x_lo": 2, "zh": 4, "zl": 4, "core": 2, "y": 4, "x_hi": 2}
ZZ = ("zh", "zl")
WIDE = ("x_lo", "zh", "zl", "core")
NARROW = ("y", "x_hi")

NEAR, MID, FAR = [0, 5, -5], [1, 6, -4, -1, 4, -6], [8, 2, 7, -3, -2, 3, -7]
OUT_HALF = [(0, z) for z in NEAR + MID] + [(1, z) for z in NEAR]
OUT_HALF += [(0, z) for z in FAR] + [(1, z) for z in MID + FAR]
SHARE = HALF // N
PER = SHARE // ROWS
OUT_ORDER = np.array([(c,) + OUT_HALF[n * PER + i] for n in range(N) for c in range(C) for i in range(PER)], np.int32)
IN_ORDER = np.array([(c, x, z) for c in range(C) for x in range(X) for z in range(Z)], np.int32)
OWNERS = np.array([(c, x, z) for x in range(X) for z in range(Z) for c in range(C)], np.int32)

VMEM = pl.BlockSpec(memory_space=pltpu.VMEM)
SMEM = pl.BlockSpec(memory_space=pltpu.SMEM)


def params():
    return pltpu.CompilerParams(vmem_limit_bytes=48 * 2**20)


def shift(x, axis, by):
    size = math.prod(AXES[a] for a in (axis if isinstance(axis, tuple) else (axis,)))
    return lax.ppermute(x, axis, [(i, (i + by) % size) for i in range(size)])


def from_z(x, distance):
    return shift(x, ZZ, -distance)


def cat(*parts):
    return jnp.concatenate(parts, 0)


def half(v):
    return v.astype(jnp.bfloat16)


def f32(v):
    return v.astype(jnp.float32)


def dot(a, b, over_a=1, over_b=0):
    return lax.dot_general(a, b, (((over_a,), (over_b,)), ((), ())), preferred_element_type=jnp.float32)


def rotate_in_kernel(at_ref, in_ref, basis_ref, keep_ref, send_ref, wide_s, rows_s):
    wide_s[:TOKENS, :] = f32(in_ref[...])
    wide_s[TOKENS:, :] = jnp.zeros((8, in_ref.shape[1]), jnp.float32)
    real = lax.broadcasted_iota(jnp.int32, (ROWS, 1), 0) < OWN
    for i in range(PIECES):
        block = jnp.where(real, wide_s[i * OWN:i * OWN + ROWS, :], 0.0)
        rows_s[pl.ds(pl.multiple_of(at_ref[i] * ROWS, ROWS), ROWS), :] = block
    for i in range(0, HALF, RUN):
        keep_ref[i:i + RUN, :] = dot(half(rows_s[i:i + RUN, :]), basis_ref[...])
        send_ref[i:i + RUN, :] = half(dot(half(rows_s[HALF + i:HALF + i + RUN, :]), basis_ref[...]))


def rotate_out_kernel(core_ref, *refs):
    blocks, (own_ref, other_ref, out_ref, rows_s) = refs[:6], refs[6:]
    at = 0
    for block in blocks:
        rows_s[at:at + block.shape[0], :] = block[...]
        at += block.shape[0]
    for i, basis in enumerate((own_ref, other_ref)):
        product = half(dot(rows_s[...], basis[...], 1, 1))
        out_ref[pl.ds((core_ref[0] ^ i) * HALF, HALF), :] = product


def stack_kernel(*refs):
    at = 0
    for block in refs[:-1]:
        refs[-1][at:at + block.shape[0], :] = block[...]
        at += block.shape[0]


def padding_sum(block):
    row = lax.rem(lax.broadcasted_iota(jnp.int32, block.shape, 0), ROWS)
    column = lax.broadcasted_iota(jnp.int32, block.shape, 1)
    return jnp.sum(jnp.where((row == OWN) & (column < 3), f32(block), 0.0), keepdims=True)


def with_terms(block, value):
    row = lax.broadcasted_iota(jnp.int32, block.shape, 0)
    column = lax.broadcasted_iota(jnp.int32, block.shape, 1)
    first = f32(half(value))
    second = f32(half(value - first))
    third = value - first - second
    terms = jnp.where(column == 0, first, jnp.where(column == 1, second, jnp.where(column == 2, third, 0.0)))
    return jnp.where(row == OWN, terms, block)


def share_kernel(parts_ref, out_ref):
    shares = []
    for c in range(C):
        total = f32(parts_ref[c * N])
        for n in range(1, N):
            total += f32(parts_ref[c * N + n])
        shares.append(total)
    share = half(jnp.concatenate(shares, 1))
    for n in range(N):
        out_ref[n] = share


def query_spans(q):
    spans = []
    for x in range(X):
        lo, hi = max(q * QTOK, x * 448), min((q + 1) * QTOK, (x + 1) * 448)
        if lo < hi:
            spans.append((x, (lo - x * 448) // 28, (hi - 1 - x * 448) // 28 + 1))
    return spans


def score_kernel(to_out_ref, to_in_ref, ro_ref, *refs):
    in_refs, (eig_ref, out_ref, ro_s, ri_s) = refs[:4], refs[4:]

    def place(scratch, at_ref, i, block):
        scratch[pl.ds(pl.multiple_of(at_ref[i] * ROWS, ROWS), ROWS), :] = block

    overall = sum(padding_sum(ref[:, :128]) for ref in in_refs)
    width = ro_ref.shape[2] // C
    for i in range(PIECES):
        n, c, at = i // (C * PER), i // PER % C, i % PER * ROWS
        place(ro_s, to_out_ref, i, ro_ref[n, at:at + ROWS, c * width:(c + 1) * width])
        at = i % Z * ROWS
        place(ri_s, to_in_ref, i, in_refs[i // Z][at:at + ROWS, :])

    def rows(ref, x, c, first, last):
        base = (x * C + c) * RUN
        return ref[base + first * ROWS:base + last * ROWS, :]

    def tokens(x, c, first, last, axis):
        shape = [1, 1]
        shape[axis] = (last - first) * ROWS
        at = lax.broadcasted_iota(jnp.int32, tuple(shape), axis)
        own = lax.rem(at, ROWS)
        return jnp.where(own < OWN, x * 448 + (first + at // ROWS) * 28 + c * OWN + own, -1)

    recip = 1.0 / (f32(eig_ref[...]) + overall * (0.1 / (FF * D)))
    scored = lax.broadcasted_iota(jnp.int32, (SCORED, 1), 0) + QUERIES * QTOK
    pick = jnp.concatenate([tokens(1, c, TRAIN_Z, Z, 1) for c in range(C)], 1) == scored
    pick = half(jnp.where(pick, 1.0, 0.0))
    train_out = dot(pick, cat(*[rows(ro_s, 1, c, TRAIN_Z, Z) for c in range(C)]))
    train_in = half(dot(pick, cat(*[rows(ri_s, 1, c, TRAIN_Z, Z) for c in range(C)])))
    scale = 1.0 / math.sqrt(QTOK * FF * D)
    for q in range(QUERIES):
        outs, ins = [], []
        for x, first, last in query_spans(q):
            for c in range(C):
                token = tokens(x, c, first, last, 0)
                keep = (token >= q * QTOK) & (token < (q + 1) * QTOK)
                outs.append(half(jnp.where(keep, f32(rows(ro_s, x, c, first, last)), 0.0)))
                ins.append(rows(ri_s, x, c, first, last))
        precond = half(dot(cat(*outs), cat(*ins), 0, 0) * recip)
        projected = dot(train_in, precond, 1, 1)
        score = jnp.sum(train_out * projected, axis=1) * scale
        for n in range(N):
            out_ref[n, q, :] = score


def stack(*blocks):
    rows = sum(b.shape[0] for b in blocks)
    shape = jax.ShapeDtypeStruct((rows,) + blocks[0].shape[1:], jnp.bfloat16)
    return pl.pallas_call(
        stack_kernel,
        out_shape=shape,
        in_specs=[VMEM] * len(blocks),
        out_specs=VMEM,
        compiler_params=params(),
        cost_estimate=pl.CostEstimate(flops=0, bytes_accessed=4 * shape.size, transcendentals=0),
    )(*blocks)


def on_device(grad_out, inputs, out_basis, in_basis, eigen_values):
    x_me, c_me = lax.axis_index("x_lo"), lax.axis_index("core")
    z_me = lax.axis_index(ZZ)
    n_out, n_in = out_basis.shape[1], in_basis.shape[1]

    def places(order, core, z):
        return ((x_me ^ order[:, 1]) * C + (core ^ order[:, 0])) * Z + lax.rem(z + order[:, 2] + Z, Z)

    own_basis = out_basis.T
    own = lax.optimization_barrier(jnp.pad(grad_out, ((0, ROWS - OWN), (0, 0))))
    above, below = from_z(own, 5), from_z(own, -5)
    to_rows = ((c_me ^ OWNERS[:, 0]) * X + (x_me ^ OWNERS[:, 1])) * Z + OWNERS[:, 2]
    keep, send = pl.pallas_call(
        rotate_in_kernel,
        out_shape=(jax.ShapeDtypeStruct((HALF, n_in), jnp.float32), jax.ShapeDtypeStruct((HALF, n_in), jnp.bfloat16)),
        in_specs=[SMEM, VMEM, VMEM],
        out_specs=(VMEM, VMEM),
        scratch_shapes=[
            pltpu.VMEM((TOKENS + 8, inputs.shape[1]), jnp.float32),
            pltpu.VMEM((ALL, inputs.shape[1]), jnp.float32),
        ],
        compiler_params=params(),
        cost_estimate=pl.CostEstimate(flops=3 * 10**8, bytes_accessed=3 * 10**6, transcendentals=0),
    )(to_rows, inputs, in_basis)
    above, below, sent, eigen_values = lax.optimization_barrier((above, below, shift(send, "core", 1), eigen_values))
    part = keep + f32(sent)
    local_sum = jnp.full((N, 128), jnp.sum(eigen_values, dtype=jnp.float32))
    narrow_sum = jnp.sum(lax.all_to_all(local_sum, NARROW, 0, 0, tiled=True)[:, 0])

    near = stack(own, above, below)
    up, down, near_x = from_z(near, 1), from_z(near, -1), shift(near, "x_lo", 1)
    across = from_z(above, 3)
    other_basis = shift(own_basis, "core", 1)
    part = half(part[:RUN] + f32(shift(half(part[RUN:]), "x_lo", 1)))
    up, down, near_x = lax.optimization_barrier((up, down, near_x))
    mid = stack(up, down)
    up = from_z(up, 1)
    part, up = lax.optimization_barrier((part, up))
    *far, mid_x, narrow_sum = lax.optimization_barrier((up, from_z(down, -1), shift(mid, "x_lo", 1), narrow_sum))
    far = stack(across, *far)
    far_x = shift(far, "x_lo", 1)
    blocks = [near, mid, near_x, far, mid_x, far_x]

    pieces = lax.all_to_all(part, ZZ, 0, 0, tiled=True)
    partial_out = pl.pallas_call(
        rotate_out_kernel,
        out_shape=jax.ShapeDtypeStruct((ALL, n_out), jnp.bfloat16),
        in_specs=[SMEM] + [VMEM] * 8,
        out_specs=VMEM,
        scratch_shapes=[pltpu.VMEM((HALF, grad_out.shape[1]), jnp.bfloat16)],
        compiler_params=params(),
        cost_estimate=pl.CostEstimate(flops=33 * 10**8, bytes_accessed=10**7, transcendentals=0),
    )(c_me.astype(jnp.int32).reshape(1), *blocks, own_basis, other_basis)
    pieces, partial_out = lax.optimization_barrier((pieces, partial_out))
    own_in = jnp.sum(f32(pieces.reshape(Z, ROWS, n_in)), 0)
    own_in = half(with_terms(own_in, narrow_sum))
    column = lax.all_gather(own_in, ZZ, axis=0, tiled=True)
    parts = lax.all_to_all(partial_out, ("core",) + NARROW, 0, 0, tiled=True)
    parts, column = lax.optimization_barrier((parts, column))
    shares = pl.pallas_call(
        share_kernel,
        out_shape=jax.ShapeDtypeStruct((N, SHARE, C * n_out), jnp.bfloat16),
        in_specs=[VMEM],
        out_specs=VMEM,
        compiler_params=params(),
        cost_estimate=pl.CostEstimate(flops=10**6, bytes_accessed=2 * 10**6, transcendentals=0),
    )(parts.reshape(C * N, SHARE, n_out))
    column_x = shift(column, "x_lo", 1)
    rotated_in = [column, column_x, shift(column, "core", 1), shift(column_x, "core", 1)]
    rotated_out = lax.all_to_all(shares, NARROW, 0, 0, tiled=True)

    scores = pl.pallas_call(
        score_kernel,
        out_shape=jax.ShapeDtypeStruct((N, QUERIES, SCORED), jnp.float32),
        in_specs=[SMEM] * 2 + [VMEM] * 6,
        out_specs=VMEM,
        scratch_shapes=[pltpu.VMEM((ALL, n_out), jnp.bfloat16), pltpu.VMEM((ALL, n_in), jnp.bfloat16)],
        compiler_params=params(),
        cost_estimate=pl.CostEstimate(flops=3 * 10**9, bytes_accessed=5 * 10**6, transcendentals=0),
    )(places(OUT_ORDER, 0, z_me), places(IN_ORDER, c_me, 0), rotated_out, *rotated_in, eigen_values)
    scores = jnp.sum(lax.all_to_all(scores, NARROW, 0, 0, tiled=True), 0)
    for axes in (("zl", "core"), ("x_lo", "zh")):
        scores = jnp.sum(lax.all_to_all(jnp.broadcast_to(scores, (8,) + scores.shape), axes, 0, 0, tiled=True), 0)
    return scores


def solution(mesh):
    fine = Mesh(mesh.devices.reshape(tuple(AXES.values())), tuple(AXES))
    return jax.shard_map(
        on_device,
        mesh=fine,
        in_specs=(
            P(WIDE, NARROW),
            P(None, WIDE),
            P(NARROW, WIDE),
            P(WIDE, NARROW),
            P(WIDE, NARROW),
        ),
        out_specs=P(),
        check_vma=False,
    )
```

```python
import math

import jax
import jax.numpy as jnp
import numpy as np
from jax import lax
from jax.experimental import pallas as pl
from jax.experimental.pallas import tpu as pltpu
from jax.sharding import Mesh, PartitionSpec as P

D = 8192
FF = 28672
QUERIES = 4
QTOK = 128
TOKENS = 896
SCORED = TOKENS - QUERIES * QTOK
X, Z, C, N = 2, 16, 2, 8
OWN = 14
ROWS = 16
RUN = Z * ROWS
HALF = X * RUN
ALL = C * HALF
PIECES = ALL // ROWS
TRAIN_Z = 2
AXES = {"x_lo": 2, "zh": 4, "zl": 4, "core": 2, "y": 4, "x_hi": 2}
ZZ = ("zh", "zl")
WIDE = ("x_lo", "zh", "zl", "core")
NARROW = ("y", "x_hi")

NEAR, MID, FAR = [0, 5, -5], [1, 6, -4, -1, 4, -6], [8, 2, 7, -3, -2, 3, -7]
OUT_HALF = [(0, z) for z in NEAR + MID] + [(1, z) for z in NEAR]
OUT_HALF += [(0, z) for z in FAR] + [(1, z) for z in MID + FAR]
SHARE = HALF // N
PER = SHARE // ROWS
OUT_ORDER = np.array([(c,) + OUT_HALF[n * PER + i] for n in range(N) for c in range(C) for i in range(PER)], np.int32)
IN_ORDER = np.array([(c, x, z) for c in range(C) for x in range(X) for z in range(Z)], np.int32)
OWNERS = np.array([(c, x, z) for x in range(X) for z in range(Z) for c in range(C)], np.int32)

VMEM = pl.BlockSpec(memory_space=pltpu.VMEM)
SMEM = pl.BlockSpec(memory_space=pltpu.SMEM)


def params():
    return pltpu.CompilerParams(vmem_limit_bytes=48 * 2**20)


def shift(x, axis, by):
    size = math.prod(AXES[a] for a in (axis if isinstance(axis, tuple) else (axis,)))
    return lax.ppermute(x, axis, [(i, (i + by) % size) for i in range(size)])


def from_z(x, distance):
    return shift(x, ZZ, -distance)


def cat(*parts):
    return jnp.concatenate(parts, 0)


def half(v):
    return v.astype(jnp.bfloat16)


def f32(v):
    return v.astype(jnp.float32)


def dot(a, b, over_a=1, over_b=0):
    return lax.dot_general(a, b, (((over_a,), (over_b,)), ((), ())), preferred_element_type=jnp.float32)


def rotate_in_kernel(at_ref, in_ref, basis_ref, keep_ref, send_ref, wide_s, rows_s):
    wide_s[:TOKENS, :] = f32(in_ref[...])
    wide_s[TOKENS:, :] = jnp.zeros((8, in_ref.shape[1]), jnp.float32)
    real = lax.broadcasted_iota(jnp.int32, (ROWS, 1), 0) < OWN
    for i in range(PIECES):
        block = jnp.where(real, wide_s[i * OWN:i * OWN + ROWS, :], 0.0)
        rows_s[pl.ds(pl.multiple_of(at_ref[i] * ROWS, ROWS), ROWS), :] = block
    for i in range(0, HALF, RUN):
        keep_ref[i:i + RUN, :] = dot(half(rows_s[i:i + RUN, :]), basis_ref[...])
        send_ref[i:i + RUN, :] = half(dot(half(rows_s[HALF + i:HALF + i + RUN, :]), basis_ref[...]))


def rotate_out_kernel(core_ref, *refs):
    blocks, (own_ref, other_ref, out_ref, rows_s) = refs[:6], refs[6:]
    at = 0
    for block in blocks:
        rows_s[at:at + block.shape[0], :] = block[...]
        at += block.shape[0]
    for i, basis in enumerate((own_ref, other_ref)):
        product = half(dot(rows_s[...], basis[...], 1, 1))
        out_ref[pl.ds((core_ref[0] ^ i) * HALF, HALF), :] = product


def stack_kernel(*refs):
    at = 0
    for block in refs[:-1]:
        refs[-1][at:at + block.shape[0], :] = block[...]
        at += block.shape[0]


def padding_sum(block):
    row = lax.rem(lax.broadcasted_iota(jnp.int32, block.shape, 0), ROWS)
    column = lax.broadcasted_iota(jnp.int32, block.shape, 1)
    return jnp.sum(jnp.where((row == OWN) & (column < 3), f32(block), 0.0), keepdims=True)


def with_terms(block, value):
    row = lax.broadcasted_iota(jnp.int32, block.shape, 0)
    column = lax.broadcasted_iota(jnp.int32, block.shape, 1)
    first = f32(half(value))
    second = f32(half(value - first))
    third = value - first - second
    terms = jnp.where(column == 0, first, jnp.where(column == 1, second, jnp.where(column == 2, third, 0.0)))
    return jnp.where(row == OWN, terms, block)


def share_kernel(parts_ref, out_ref):
    shares = []
    for c in range(C):
        total = f32(parts_ref[c * N])
        for n in range(1, N):
            total += f32(parts_ref[c * N + n])
        shares.append(total)
    share = half(jnp.concatenate(shares, 1))
    for n in range(N):
        out_ref[n] = share


def query_spans(q):
    spans = []
    for x in range(X):
        lo, hi = max(q * QTOK, x * 448), min((q + 1) * QTOK, (x + 1) * 448)
        if lo < hi:
            spans.append((x, (lo - x * 448) // 28, (hi - 1 - x * 448) // 28 + 1))
    return spans


def score_kernel(to_out_ref, to_in_ref, ro_ref, *refs):
    in_refs, (eig_ref, out_ref, ro_s, ri_s) = refs[:4], refs[4:]

    def place(scratch, at_ref, i, block):
        scratch[pl.ds(pl.multiple_of(at_ref[i] * ROWS, ROWS), ROWS), :] = block

    overall = sum(padding_sum(ref[:, :128]) for ref in in_refs)
    width = ro_ref.shape[2] // C
    for i in range(PIECES):
        n, c, at = i // (C * PER), i // PER % C, i % PER * ROWS
        place(ro_s, to_out_ref, i, ro_ref[n, at:at + ROWS, c * width:(c + 1) * width])
        at = i % Z * ROWS
        place(ri_s, to_in_ref, i, in_refs[i // Z][at:at + ROWS, :])

    def rows(ref, x, c, first, last):
        base = (x * C + c) * RUN
        return ref[base + first * ROWS:base + last * ROWS, :]

    def tokens(x, c, first, last, axis):
        shape = [1, 1]
        shape[axis] = (last - first) * ROWS
        at = lax.broadcasted_iota(jnp.int32, tuple(shape), axis)
        own = lax.rem(at, ROWS)
        return jnp.where(own < OWN, x * 448 + (first + at // ROWS) * 28 + c * OWN + own, -1)

    recip = 1.0 / (f32(eig_ref[...]) + overall * (0.1 / (FF * D)))
    scored = lax.broadcasted_iota(jnp.int32, (SCORED, 1), 0) + QUERIES * QTOK
    pick = jnp.concatenate([tokens(1, c, TRAIN_Z, Z, 1) for c in range(C)], 1) == scored
    pick = half(jnp.where(pick, 1.0, 0.0))
    train_out = dot(pick, cat(*[rows(ro_s, 1, c, TRAIN_Z, Z) for c in range(C)]))
    train_in = half(dot(pick, cat(*[rows(ri_s, 1, c, TRAIN_Z, Z) for c in range(C)])))
    scale = 1.0 / math.sqrt(QTOK * FF * D)
    for q in range(QUERIES):
        outs, ins = [], []
        for x, first, last in query_spans(q):
            for c in range(C):
                token = tokens(x, c, first, last, 0)
                keep = (token >= q * QTOK) & (token < (q + 1) * QTOK)
                outs.append(half(jnp.where(keep, f32(rows(ro_s, x, c, first, last)), 0.0)))
                ins.append(rows(ri_s, x, c, first, last))
        precond = half(dot(cat(*outs), cat(*ins), 0, 0) * recip)
        projected = dot(train_in, precond, 1, 1)
        score = jnp.sum(train_out * projected, axis=1) * scale
        for n in range(N):
            out_ref[n, q, :] = score


def stack(*blocks):
    rows = sum(b.shape[0] for b in blocks)
    shape = jax.ShapeDtypeStruct((rows,) + blocks[0].shape[1:], jnp.bfloat16)
    return pl.pallas_call(
        stack_kernel,
        out_shape=shape,
        in_specs=[VMEM] * len(blocks),
        out_specs=VMEM,
        compiler_params=params(),
        cost_estimate=pl.CostEstimate(flops=0, bytes_accessed=4 * shape.size, transcendentals=0),
    )(*blocks)


def on_device(grad_out, inputs, out_basis, in_basis, eigen_values):
    x_me, c_me = lax.axis_index("x_lo"), lax.axis_index("core")
    z_me = lax.axis_index(ZZ)
    n_out, n_in = out_basis.shape[1], in_basis.shape[1]

    def places(order, core, z):
        return ((x_me ^ order[:, 1]) * C + (core ^ order[:, 0])) * Z + lax.rem(z + order[:, 2] + Z, Z)

    own_basis = out_basis.T
    own = lax.optimization_barrier(jnp.pad(grad_out, ((0, ROWS - OWN), (0, 0))))
    above, below = from_z(own, 5), from_z(own, -5)
    to_rows = ((c_me ^ OWNERS[:, 0]) * X + (x_me ^ OWNERS[:, 1])) * Z + OWNERS[:, 2]
    keep, send = pl.pallas_call(
        rotate_in_kernel,
        out_shape=(jax.ShapeDtypeStruct((HALF, n_in), jnp.float32), jax.ShapeDtypeStruct((HALF, n_in), jnp.bfloat16)),
        in_specs=[SMEM, VMEM, VMEM],
        out_specs=(VMEM, VMEM),
        scratch_shapes=[
            pltpu.VMEM((TOKENS + 8, inputs.shape[1]), jnp.float32),
            pltpu.VMEM((ALL, inputs.shape[1]), jnp.float32),
        ],
        compiler_params=params(),
        cost_estimate=pl.CostEstimate(flops=3 * 10**8, bytes_accessed=3 * 10**6, transcendentals=0),
    )(to_rows, inputs, in_basis)
    above, below, sent, eigen_values = lax.optimization_barrier((above, below, shift(send, "core", 1), eigen_values))
    part = keep + f32(sent)
    local_sum = jnp.full((N, 128), jnp.sum(eigen_values, dtype=jnp.float32))
    narrow_sum = jnp.sum(lax.all_to_all(local_sum, NARROW, 0, 0, tiled=True)[:, 0])

    near = stack(own, above, below)
    up, down, near_x = from_z(near, 1), from_z(near, -1), shift(near, "x_lo", 1)
    across = from_z(above, 3)
    part = half(part[:RUN] + f32(shift(half(part[RUN:]), "x_lo", 1)))
    up, down, near_x, narrow_sum, own_basis = lax.optimization_barrier((up, down, near_x, narrow_sum, own_basis))
    other_basis = shift(own_basis, "core", 1)
    mid = stack(up, down)
    across, *far, mid_x, part = lax.optimization_barrier(
        (across, from_z(up, 1), from_z(down, -1), shift(mid, "x_lo", 1), part)
    )
    far = stack(across, *far)
    far_x = shift(far, "x_lo", 1)
    blocks = [near, mid, near_x, far, mid_x, far_x]

    pieces = lax.all_to_all(part, ZZ, 0, 0, tiled=True)
    partial_out = pl.pallas_call(
        rotate_out_kernel,
        out_shape=jax.ShapeDtypeStruct((ALL, n_out), jnp.bfloat16),
        in_specs=[SMEM] + [VMEM] * 8,
        out_specs=VMEM,
        scratch_shapes=[pltpu.VMEM((HALF, grad_out.shape[1]), jnp.bfloat16)],
        compiler_params=params(),
        cost_estimate=pl.CostEstimate(flops=33 * 10**8, bytes_accessed=10**7, transcendentals=0),
    )(c_me.astype(jnp.int32).reshape(1), *blocks, own_basis, other_basis)
    pieces, partial_out = lax.optimization_barrier((pieces, partial_out))
    own_in = jnp.sum(f32(pieces.reshape(Z, ROWS, n_in)), 0)
    own_in = half(with_terms(own_in, narrow_sum))
    column = lax.all_gather(own_in, ZZ, axis=0, tiled=True)
    parts = lax.all_to_all(partial_out, ("core",) + NARROW, 0, 0, tiled=True)
    parts, column = lax.optimization_barrier((parts, column))
    shares = pl.pallas_call(
        share_kernel,
        out_shape=jax.ShapeDtypeStruct((N, SHARE, C * n_out), jnp.bfloat16),
        in_specs=[VMEM],
        out_specs=VMEM,
        compiler_params=params(),
        cost_estimate=pl.CostEstimate(flops=10**6, bytes_accessed=2 * 10**6, transcendentals=0),
    )(parts.reshape(C * N, SHARE, n_out))
    column_x = shift(column, "x_lo", 1)
    rotated_in = [column, column_x, shift(column, "core", 1), shift(column_x, "core", 1)]
    rotated_out = lax.all_to_all(shares, NARROW, 0, 0, tiled=True)

    scores = pl.pallas_call(
        score_kernel,
        out_shape=jax.ShapeDtypeStruct((N, QUERIES, SCORED), jnp.float32),
        in_specs=[SMEM] * 2 + [VMEM] * 6,
        out_specs=VMEM,
        scratch_shapes=[pltpu.VMEM((ALL, n_out), jnp.bfloat16), pltpu.VMEM((ALL, n_in), jnp.bfloat16)],
        compiler_params=params(),
        cost_estimate=pl.CostEstimate(flops=3 * 10**9, bytes_accessed=5 * 10**6, transcendentals=0),
    )(places(OUT_ORDER, 0, z_me), places(IN_ORDER, c_me, 0), rotated_out, *rotated_in, eigen_values)
    scores = jnp.sum(lax.all_to_all(scores, NARROW, 0, 0, tiled=True), 0)
    for axes in (("zl", "core"), ("x_lo", "zh")):
        scores = jnp.sum(lax.all_to_all(jnp.broadcast_to(scores, (8,) + scores.shape), axes, 0, 0, tiled=True), 0)
    return scores


def solution(mesh):
    fine = Mesh(mesh.devices.reshape(tuple(AXES.values())), tuple(AXES))
    return jax.shard_map(
        on_device,
        mesh=fine,
        in_specs=(
            P(WIDE, NARROW),
            P(None, WIDE),
            P(NARROW, WIDE),
            P(WIDE, NARROW),
            P(WIDE, NARROW),
        ),
        out_specs=P(),
        check_vma=False,
    )
```

```python
import math

import jax
import jax.numpy as jnp
import numpy as np
from jax import lax
from jax.experimental import pallas as pl
from jax.experimental.pallas import tpu as pltpu
from jax.sharding import Mesh, PartitionSpec as P

D = 8192
FF = 28672
QUERIES = 4
QTOK = 128
TOKENS = 896
SCORED = TOKENS - QUERIES * QTOK
X, Z, C, N = 2, 16, 2, 8
OWN = 14
ROWS = 16
RUN = Z * ROWS
HALF = X * RUN
ALL = C * HALF
PIECES = ALL // ROWS
TRAIN_Z = 2
AXES = {"x_lo": 2, "zh": 4, "zl": 4, "core": 2, "y": 4, "x_hi": 2}
ZZ = ("zh", "zl")
WIDE = ("x_lo", "zh", "zl", "core")
NARROW = ("y", "x_hi")

NEAR, MID, FAR = [0, 5, -5], [1, 6, -4, -1, 4, -6], [8, 2, 7, -3, -2, 3, -7]
OUT_HALF = [(0, z) for z in NEAR + MID] + [(1, z) for z in NEAR]
OUT_HALF += [(0, z) for z in FAR] + [(1, z) for z in MID + FAR]
SHARE = HALF // N
PER = SHARE // ROWS
OUT_ORDER = np.array([(c,) + OUT_HALF[n * PER + i] for n in range(N) for c in range(C) for i in range(PER)], np.int32)
IN_ORDER = np.array([(c, x, z) for c in range(C) for x in range(X) for z in range(Z)], np.int32)
OWNERS = np.array([(c, x, z) for x in range(X) for z in range(Z) for c in range(C)], np.int32)

VMEM = pl.BlockSpec(memory_space=pltpu.VMEM)
SMEM = pl.BlockSpec(memory_space=pltpu.SMEM)


def params():
    return pltpu.CompilerParams(vmem_limit_bytes=48 * 2**20)


def shift(x, axis, by):
    size = math.prod(AXES[a] for a in (axis if isinstance(axis, tuple) else (axis,)))
    return lax.ppermute(x, axis, [(i, (i + by) % size) for i in range(size)])


def from_z(x, distance):
    return shift(x, ZZ, -distance)


def cat(*parts):
    return jnp.concatenate(parts, 0)


def half(v):
    return v.astype(jnp.bfloat16)


def f32(v):
    return v.astype(jnp.float32)


def dot(a, b, over_a=1, over_b=0):
    return lax.dot_general(a, b, (((over_a,), (over_b,)), ((), ())), preferred_element_type=jnp.float32)


def own_kernel(grad_ref, eig_ref, out_ref):
    value = jnp.sum(f32(eig_ref[...]), keepdims=True)
    padding = jnp.zeros((ROWS - OWN, grad_ref.shape[1]), jnp.float32)
    out_ref[...] = half(with_terms(cat(f32(grad_ref[...]), padding), value, ROWS))


def rotate_in_kernel(at_ref, in_ref, basis_ref, keep_ref, send_ref, wide_s, rows_s):
    wide_s[:TOKENS, :] = f32(in_ref[...])
    wide_s[TOKENS:, :] = jnp.zeros((8, in_ref.shape[1]), jnp.float32)
    real = lax.broadcasted_iota(jnp.int32, (ROWS, 1), 0) < OWN
    for i in range(PIECES):
        block = jnp.where(real, wide_s[i * OWN:i * OWN + ROWS, :], 0.0)
        rows_s[pl.ds(pl.multiple_of(at_ref[i] * ROWS, ROWS), ROWS), :] = block
    for i in range(0, HALF, RUN):
        keep_ref[i:i + RUN, :] = dot(half(rows_s[i:i + RUN, :]), basis_ref[...])
        send_ref[i:i + RUN, :] = half(dot(half(rows_s[HALF + i:HALF + i + RUN, :]), basis_ref[...]))


def rotate_out_kernel(core_ref, *refs):
    blocks, (own_ref, other_ref, out_ref, rows_s) = refs[:6], refs[6:]
    at = 0
    for block in blocks:
        rows_s[at:at + block.shape[0], :] = block[...]
        at += block.shape[0]
    column_sum = padding_sum(rows_s[:, :128])
    for i, basis in enumerate((own_ref, other_ref)):
        product = with_terms(dot(rows_s[...], basis[...], 1, 1), column_sum, SHARE)
        out_ref[pl.ds((core_ref[0] ^ i) * HALF, HALF), :] = half(product)


def stack_kernel(*refs):
    at = 0
    for block in refs[:-1]:
        refs[-1][at:at + block.shape[0], :] = block[...]
        at += block.shape[0]


def padding_sum(block):
    row = lax.rem(lax.broadcasted_iota(jnp.int32, block.shape, 0), ROWS)
    column = lax.broadcasted_iota(jnp.int32, block.shape, 1)
    return jnp.sum(jnp.where((row == OWN) & (column < 3), f32(block), 0.0), keepdims=True)


def with_terms(block, value, every):
    row = lax.broadcasted_iota(jnp.int32, block.shape, 0)
    column = lax.broadcasted_iota(jnp.int32, block.shape, 1)
    first = f32(half(value))
    second = f32(half(value - first))
    third = value - first - second
    terms = jnp.where(column == 0, first, jnp.where(column == 1, second, jnp.where(column == 2, third, 0.0)))
    return jnp.where(lax.rem(row, every) == OWN, terms, block)


def share_kernel(parts_ref, out_ref, overall_ref):
    overall = sum(padding_sum(parts_ref[i, :ROWS, :128]) for i in range(C * N))
    overall_ref[...] = jnp.broadcast_to(overall, overall_ref.shape)
    shares = []
    for c in range(C):
        total = f32(parts_ref[c * N])
        for n in range(1, N):
            total += f32(parts_ref[c * N + n])
        shares.append(total)
    share = half(jnp.concatenate(shares, 1))
    for n in range(N):
        out_ref[n] = share


def query_spans(q):
    spans = []
    for x in range(X):
        lo, hi = max(q * QTOK, x * 448), min((q + 1) * QTOK, (x + 1) * 448)
        if lo < hi:
            spans.append((x, (lo - x * 448) // 28, (hi - 1 - x * 448) // 28 + 1))
    return spans


def score_kernel(to_out_ref, to_in_ref, overall_ref, ro_ref, *refs):
    in_refs, (eig_ref, out_ref, ro_s, ri_s) = refs[:4], refs[4:]

    def place(scratch, at_ref, i, block):
        scratch[pl.ds(pl.multiple_of(at_ref[i] * ROWS, ROWS), ROWS), :] = block

    overall = overall_ref[:1, :1]
    width = ro_ref.shape[2] // C
    for i in range(PIECES):
        n, c, at = i // (C * PER), i // PER % C, i % PER * ROWS
        place(ro_s, to_out_ref, i, ro_ref[n, at:at + ROWS, c * width:(c + 1) * width])
        at = i % Z * ROWS
        place(ri_s, to_in_ref, i, in_refs[i // Z][at:at + ROWS, :])

    def rows(ref, x, c, first, last):
        base = (x * C + c) * RUN
        return ref[base + first * ROWS:base + last * ROWS, :]

    def tokens(x, c, first, last, axis):
        shape = [1, 1]
        shape[axis] = (last - first) * ROWS
        at = lax.broadcasted_iota(jnp.int32, tuple(shape), axis)
        own = lax.rem(at, ROWS)
        return jnp.where(own < OWN, x * 448 + (first + at // ROWS) * 28 + c * OWN + own, -1)

    recip = 1.0 / (f32(eig_ref[...]) + overall * (0.1 / (FF * D)))
    scored = lax.broadcasted_iota(jnp.int32, (SCORED, 1), 0) + QUERIES * QTOK
    pick = jnp.concatenate([tokens(1, c, TRAIN_Z, Z, 1) for c in range(C)], 1) == scored
    pick = half(jnp.where(pick, 1.0, 0.0))
    train_out = dot(pick, cat(*[rows(ro_s, 1, c, TRAIN_Z, Z) for c in range(C)]))
    train_in = half(dot(pick, cat(*[rows(ri_s, 1, c, TRAIN_Z, Z) for c in range(C)])))
    scale = 1.0 / math.sqrt(QTOK * FF * D)
    for q in range(QUERIES):
        outs, ins = [], []
        for x, first, last in query_spans(q):
            for c in range(C):
                token = tokens(x, c, first, last, 0)
                keep = (token >= q * QTOK) & (token < (q + 1) * QTOK)
                outs.append(half(jnp.where(keep, f32(rows(ro_s, x, c, first, last)), 0.0)))
                ins.append(rows(ri_s, x, c, first, last))
        precond = half(dot(cat(*outs), cat(*ins), 0, 0) * recip)
        projected = dot(train_in, precond, 1, 1)
        score = jnp.sum(train_out * projected, axis=1) * scale
        for n in range(N):
            out_ref[n, q, :] = score


def stack(*blocks):
    rows = sum(b.shape[0] for b in blocks)
    shape = jax.ShapeDtypeStruct((rows,) + blocks[0].shape[1:], jnp.bfloat16)
    return pl.pallas_call(
        stack_kernel,
        out_shape=shape,
        in_specs=[VMEM] * len(blocks),
        out_specs=VMEM,
        compiler_params=params(),
        cost_estimate=pl.CostEstimate(flops=0, bytes_accessed=4 * shape.size, transcendentals=0),
    )(*blocks)


def on_device(grad_out, inputs, out_basis, in_basis, eigen_values):
    x_me, c_me = lax.axis_index("x_lo"), lax.axis_index("core")
    z_me = lax.axis_index(ZZ)
    n_out, n_in = out_basis.shape[1], in_basis.shape[1]

    def places(order, core, z):
        return ((x_me ^ order[:, 1]) * C + (core ^ order[:, 0])) * Z + lax.rem(z + order[:, 2] + Z, Z)

    own_basis = out_basis.T
    own = pl.pallas_call(
        own_kernel,
        out_shape=jax.ShapeDtypeStruct((ROWS, grad_out.shape[1]), jnp.bfloat16),
        in_specs=[VMEM] * 2,
        out_specs=VMEM,
        compiler_params=params(),
        cost_estimate=pl.CostEstimate(flops=10**6, bytes_accessed=10**6, transcendentals=0),
    )(grad_out, eigen_values)
    above, below = from_z(own, 5), from_z(own, -5)
    to_rows = ((c_me ^ OWNERS[:, 0]) * X + (x_me ^ OWNERS[:, 1])) * Z + OWNERS[:, 2]
    keep, send = pl.pallas_call(
        rotate_in_kernel,
        out_shape=(jax.ShapeDtypeStruct((HALF, n_in), jnp.float32), jax.ShapeDtypeStruct((HALF, n_in), jnp.bfloat16)),
        in_specs=[SMEM, VMEM, VMEM],
        out_specs=(VMEM, VMEM),
        scratch_shapes=[
            pltpu.VMEM((TOKENS + 8, inputs.shape[1]), jnp.float32),
            pltpu.VMEM((ALL, inputs.shape[1]), jnp.float32),
        ],
        compiler_params=params(),
        cost_estimate=pl.CostEstimate(flops=3 * 10**8, bytes_accessed=3 * 10**6, transcendentals=0),
    )(to_rows, inputs, in_basis)
    above, below, sent = lax.optimization_barrier((above, below, shift(send, "core", 1)))
    part = keep + f32(sent)

    near = stack(own, above, below)
    up, down, near_x = from_z(near, 1), from_z(near, -1), shift(near, "x_lo", 1)
    across = from_z(above, 3)
    part = half(part[:RUN] + f32(shift(half(part[RUN:]), "x_lo", 1)))
    up, down, near_x, across, part = lax.optimization_barrier((up, down, near_x, across, part))
    mid = stack(up, down)
    *far, mid_x, part, own_basis = lax.optimization_barrier(
        (from_z(up, 1), from_z(down, -1), shift(mid, "x_lo", 1), part, own_basis)
    )
    other_basis = shift(own_basis, "core", 1)
    far = stack(across, *far)
    far_x = shift(far, "x_lo", 1)
    blocks = [near, mid, near_x, far, mid_x, far_x]

    pieces = lax.all_to_all(part, ZZ, 0, 0, tiled=True)
    partial_out = pl.pallas_call(
        rotate_out_kernel,
        out_shape=jax.ShapeDtypeStruct((ALL, n_out), jnp.bfloat16),
        in_specs=[SMEM] + [VMEM] * 8,
        out_specs=VMEM,
        scratch_shapes=[pltpu.VMEM((HALF, grad_out.shape[1]), jnp.bfloat16)],
        compiler_params=params(),
        cost_estimate=pl.CostEstimate(flops=33 * 10**8, bytes_accessed=10**7, transcendentals=0),
    )(c_me.astype(jnp.int32).reshape(1), *blocks, own_basis, other_basis)
    pieces, partial_out = lax.optimization_barrier((pieces, partial_out))
    own_in = half(jnp.sum(f32(pieces.reshape(Z, ROWS, n_in)), 0))
    column = lax.all_gather(own_in, ZZ, axis=0, tiled=True)
    parts = lax.all_to_all(partial_out, ("core",) + NARROW, 0, 0, tiled=True)
    parts, column = lax.optimization_barrier((parts, column))
    shares, overall = pl.pallas_call(
        share_kernel,
        out_shape=(
            jax.ShapeDtypeStruct((N, SHARE, C * n_out), jnp.bfloat16),
            jax.ShapeDtypeStruct((8, 128), jnp.float32),
        ),
        in_specs=[VMEM],
        out_specs=(VMEM, VMEM),
        compiler_params=params(),
        cost_estimate=pl.CostEstimate(flops=10**6, bytes_accessed=2 * 10**6, transcendentals=0),
    )(parts.reshape(C * N, SHARE, n_out))
    column_x = shift(column, "x_lo", 1)
    rotated_in = [column, column_x, shift(column, "core", 1), shift(column_x, "core", 1)]
    rotated_out = lax.all_to_all(shares, NARROW, 0, 0, tiled=True)

    scores = pl.pallas_call(
        score_kernel,
        out_shape=jax.ShapeDtypeStruct((N, QUERIES, SCORED), jnp.float32),
        in_specs=[SMEM] * 2 + [VMEM] * 7,
        out_specs=VMEM,
        scratch_shapes=[pltpu.VMEM((ALL, n_out), jnp.bfloat16), pltpu.VMEM((ALL, n_in), jnp.bfloat16)],
        compiler_params=params(),
        cost_estimate=pl.CostEstimate(flops=3 * 10**9, bytes_accessed=5 * 10**6, transcendentals=0),
    )(places(OUT_ORDER, 0, z_me), places(IN_ORDER, c_me, 0), overall, rotated_out, *rotated_in, eigen_values)
    scores = jnp.sum(lax.all_to_all(scores, NARROW, 0, 0, tiled=True), 0)
    for axes in (("zl", "core"), ("x_lo", "zh")):
        scores = jnp.sum(lax.all_to_all(jnp.broadcast_to(scores, (8,) + scores.shape), axes, 0, 0, tiled=True), 0)
    return scores


def solution(mesh):
    fine = Mesh(mesh.devices.reshape(tuple(AXES.values())), tuple(AXES))
    return jax.shard_map(
        on_device,
        mesh=fine,
        in_specs=(
            P(WIDE, NARROW),
            P(None, WIDE),
            P(NARROW, WIDE),
            P(WIDE, NARROW),
            P(WIDE, NARROW),
        ),
        out_specs=P(),
        check_vma=False,
    )
```
